512 devices in a mesh: band: 16 (over x, z_lo), mesh: 32 (over z_hi, y, core).
Axes of the slice: x: 4, y: 4, z: 16 (z_hi: 4, z_lo: 4; z = z_hi * 4 + z_lo), core: 2. Of those that a mesh axis runs over, the one named last changes fastest.
Arguments:
- vectors: float32 [512, 65536], P('band', 'mesh'), may hold values from -6 to 6
- potential: float32 [65536], P('mesh'), may hold values from 0.5 to 3
- cell_scale: float32 [256], P('mesh'), may hold values from 0.5 to 2
- cell_matrix: float32 [343, 343], replicated, may hold values from -1 to 2, as said below
- cell_nodes: int32 [256, 343], P('mesh'), may hold values from 0 to 2559, as said below
- send_list: int32 [32, 4, 128], P('mesh'), may hold values from 0 to 2047, as said below
- node_count: int32 [32], P('mesh'), may hold values from 1024 to 2048, as said below
- filter_bounds: float32 [3], replicated, may hold values from -1 to 30, as said below
Outputs:
- filtered: float32 [512, 65536], P('band', 'mesh')
- hproj: float32 [512, 512], P('band')
The draws below stay inside these ranges and needn't reach their ends.
Inputs may be any that keep to these rules, and one draw needn't show every extreme that they name: Partition p's live nodes are its local indices below node_count[p]; some partition has all 2048 live. send_list[q, k, :] are distinct live local nodes of partition q, sent to partition (q - o_k) mod 32 with o = (-2, -1, 1, 2). `cell_nodes`: entries below 2048 are live nodes of the cell's own partition; the others are ghost slots 2048 + k * 128 + s as in the reference program. `cell_matrix`: symmetric. filter_bounds[0] lies in [-1, 0], filter_bounds[1] in [6, 8], filter_bounds[2] in [24, 30].
All inputs are finite; a program needn't handle non-finite values.
Results may differ from the reference program's by a relative error of at most 0.0001.
Values sent between devices are 32-bit elements; how exact they have to be, the bound alone decides.
No kernel may reach another device: no remote copies, remote signals or barrier semaphores. Data moves between devices by JAX's collectives and lax.ppermute only.
A program may use at most 64 MiB of HBM per device.

```python
import math
import jax
import jax.numpy as jnp
from jax import lax

NPC = 343
DEGREE = 3
CELL_DEV = 8
NODE_DEV = 2048
SLOTS = 128
BANDS = 512
NODES = 65536
CELLS = 256
N_BAND = 16
N_MESH = 32


def layout(key):
    counts = jax.random.randint(jax.random.fold_in(key, 11), (N_MESH,), NODE_DEV // 2, NODE_DEV + 1)
    fullest = jax.random.randint(jax.random.fold_in(key, 12), (), 0, N_MESH)
    counts = jnp.where(jnp.arange(N_MESH) == fullest, NODE_DEV, counts).astype(jnp.int32)
    positions = jnp.arange(NODE_DEV, dtype=jnp.int32)
    scores = jax.random.randint(jax.random.fold_in(key, 13), (N_MESH, 4, NODE_DEV), 0, (1 << 30) // NODE_DEV) * NODE_DEV + positions
    is_live = positions[None, None, :] < counts[:, None, None]
    scores = jnp.where(is_live, scores, -1 - positions[None, None, :])
    forced = 1 << 30
    first_list = (jnp.arange(4) == 0)[None, :, None]
    second_list = (jnp.arange(4) == 1)[None, :, None]
    scores = jnp.where(first_list & (positions[None, None, :] == counts[:, None, None] - 1), forced, scores)
    scores = jnp.where(second_list & (positions[None, None, :] == 0), forced, scores)
    send_rows = lax.top_k(scores, SLOTS)[1].astype(jnp.int32)
    cell_total = N_MESH * CELL_DEV
    cell_owner = jnp.arange(cell_total, dtype=jnp.int32) // CELL_DEV
    own_ids = jax.random.randint(jax.random.fold_in(key, 14), (cell_total, NPC), 0, counts[cell_owner][:, None])
    ghost_ids = NODE_DEV + jax.random.randint(jax.random.fold_in(key, 15), (cell_total, NPC), 0, 4 * SLOTS)
    is_ghost = jax.random.randint(jax.random.fold_in(key, 16), (cell_total, NPC), 0, 5) == 0
    node_ids = jnp.where(is_ghost, ghost_ids, own_ids)
    first_cell = (jnp.arange(cell_total) % CELL_DEV == 0)[:, None]
    node_ids = jnp.where(first_cell & (jnp.arange(NPC) == 0)[None, :], NODE_DEV + 4 * SLOTS - 1, node_ids)
    node_ids = jnp.where(first_cell & (jnp.arange(NPC) == 1)[None, :], 0, node_ids)
    return (counts, send_rows, node_ids.astype(jnp.int32))


def draw_node_count(key, part):
    return layout(key)[0]


def draw_send_list(key, part):
    return layout(key)[1]


def draw_cell_nodes(key, part):
    return layout(key)[2]


def draw_cell_matrix(key, part):
    key = jax.random.fold_in(key, 31)
    noise = jax.random.normal(jax.random.fold_in(key, 1), (NPC, NPC), jnp.float32)
    coupling = (noise + noise.T) * (0.35 / math.sqrt(NPC))
    diagonal_part = jax.random.uniform(jax.random.fold_in(key, 2), (NPC,), jnp.float32, 1.0, 2.0)
    identity = jnp.eye(NPC, dtype=jnp.float32)
    return coupling * (1.0 - identity) + identity * diagonal_part[None, :]


def draw_filter_bounds(key, part):
    key = jax.random.fold_in(key, 41)
    fractions = jax.random.uniform(key, (3,), jnp.float32, 0.0, 1.0)
    return jnp.stack([-1.0 + fractions[0], 6.0 + 2.0 * fractions[1], 24.0 + 6.0 * fractions[2]])


def level_of(own_key, extent, shards, smallest, largest):
    def one(position, parts):
        heights = jax.random.uniform(jax.random.fold_in(jax.random.fold_in(own_key, 6), position), (parts,), jnp.float32, smallest / len(shards), largest / len(shards))
        return jnp.repeat(jnp.exp(heights), extent[position] // parts).reshape((-1,) + (1,) * (len(extent) - position - 1))

    level = one(*shards[0])
    for cut in shards[1:]:
        level = level * one(*cut)
    return level


def scatter_about(stream_key, shape, deviation, limit, split=(), held_as=jnp.bfloat16):
    level = level_of(stream_key, shape, split, -0.22, 0.18) if split else 1.0
    result = jax.random.normal(stream_key, shape, jnp.float32) * deviation * level
    return jnp.minimum(jnp.maximum(result, -limit), limit).astype(held_as)


def setup_inputs(seed: int = 0) -> dict:
    key_of = jax.random.split(jax.random.key(seed), 9)
    vectors = scatter_about(key_of[0], (BANDS, NODES), 1.0, 6.0, ((0, 16), (1, 32)), jnp.float32)
    potential = jnp.clip(0.5 + 2.5 * jax.random.uniform(key_of[1], (NODES,), jnp.float32) ** level_of(key_of[1], (NODES,), ((0, 32),), -0.2, 0.2), 0.5, 3.0)
    cell_scale = jnp.clip(jnp.exp(math.log(2.0) - 1.3862944 * jax.random.uniform(key_of[2], (CELLS,), jnp.float32) ** level_of(key_of[2], (CELLS,), ((0, 32),), -0.2, 0.2)), 0.5, 2.0)
    cell_matrix = draw_cell_matrix(jax.random.fold_in(key_of[8], 71), 0)
    cell_nodes = draw_cell_nodes(jax.random.fold_in(key_of[8], 71), 0)
    send_list = draw_send_list(jax.random.fold_in(key_of[8], 71), 0)
    node_count = draw_node_count(jax.random.fold_in(key_of[8], 71), 0)
    filter_bounds = draw_filter_bounds(jax.random.fold_in(key_of[8], 71), 0)
    return {"vectors": vectors, "potential": potential, "cell_scale": cell_scale, "cell_matrix": cell_matrix, "cell_nodes": cell_nodes, "send_list": send_list, "node_count": node_count, "filter_bounds": filter_bounds}


OFFSETS = (-2, -1, 1, 2)
HIGHEST = lax.Precision.HIGHEST


def filter_pass(vectors, operator, filter_bounds):
    lowest = filter_bounds[0]
    wanted_top = filter_bounds[1]
    upper = filter_bounds[2]
    half_width = (upper - wanted_top) / 2.0
    centre = (upper + wanted_top) / 2.0
    sigma_now = half_width / (lowest - centre)
    gamma_ratio = 2.0 / sigma_now
    previous = vectors
    current = (sigma_now / half_width) * (operator(vectors) - centre * vectors)
    for degree_step in range(DEGREE - 1):
        sigma_next = 1.0 / (gamma_ratio - sigma_now)
        following = (2.0 * sigma_next / half_width) * (operator(current) - centre * current) - (sigma_now * sigma_next) * previous
        previous = current
        current = following
        sigma_now = sigma_next
    return current


def reference(vectors, potential, cell_scale, cell_matrix, cell_nodes, send_list, node_count, filter_bounds):
    band_total = vectors.shape[0]
    node_total = vectors.shape[1]
    node_width = node_total // N_MESH
    cell_owner = (jnp.arange(cell_nodes.shape[0], dtype=jnp.int32) // CELL_DEV)[:, None]
    ghost_pos = jnp.maximum(cell_nodes - node_width, 0).astype(jnp.int32)
    which_list = jnp.minimum(ghost_pos // SLOTS, 3).astype(jnp.int32)
    slot_pos = (ghost_pos % SLOTS).astype(jnp.int32)
    offset_table = jnp.array(OFFSETS, dtype=jnp.int32)
    source_part = ((cell_owner + offset_table[which_list]) % N_MESH).astype(jnp.int32)
    remote_ids = source_part * node_width + send_list[source_part, which_list, slot_pos]
    global_ids = jnp.where(cell_nodes < node_width, cell_owner * node_width + cell_nodes, remote_ids)
    global_ids = global_ids.astype(jnp.int32).reshape(-1)
    positions = jnp.arange(node_total, dtype=jnp.int32)
    is_live = (positions % node_width) < node_count[positions // node_width]
    start_vectors = jnp.where(is_live[None, :], vectors, jnp.zeros_like(vectors))

    def apply_rows(band_rows):
        row_count = band_rows.shape[0]
        cell_values = band_rows[:, global_ids].reshape(row_count, -1, NPC)
        products = jnp.einsum("bcn,nm->bcm", cell_values, cell_matrix, precision=HIGHEST) * cell_scale[None, :, None]
        sums = jnp.zeros_like(band_rows).at[:, global_ids].add(products.reshape(row_count, -1))
        return sums + potential[None, :] * band_rows

    def operator(field):
        blocks = field.reshape(N_BAND, band_total // N_BAND, node_total)
        return lax.map(apply_rows, blocks).reshape(band_total, node_total)

    filtered = filter_pass(start_vectors, operator, filter_bounds)
    filtered = filter_pass(filtered, operator, filter_bounds)
    applied = operator(filtered)
    hproj = lax.dot_general(applied, filtered, (((1,), (1,)), ((), ())), precision=HIGHEST) / node_total
    return filtered, hproj
```

```python
import jax
import jax.numpy as jnp
from jax import lax
from jax.experimental import pallas as pl
from jax.experimental.pallas import tpu as pltpu
from jax.sharding import PartitionSpec as P

DEGREE = 3
OFFSETS = (-2, -1, 1, 2)
HIGHEST = lax.Precision.HIGHEST

PARTS = 32
GROUPS = PARTS // 8
NODES = 2048
SLOTS = 128
GHOSTS = 4 * SLOTS
EXT = GHOSTS + NODES
CELLS = 8
NPC = 343
NPC_PAD = 384
CELL_CHUNKS = NPC_PAD // 128
ENTRIES = CELLS * NPC + GHOSTS
ENTRY_CHUNKS = 26
ENTRY_PAD = ENTRY_CHUNKS * 128
PAD_KEY = 4000

IDX_AT = 0
POS_AT = IDX_AT + CELLS * CELL_CHUNKS
KEY_AT = POS_AT + ENTRY_CHUNKS
END_AT = KEY_AT + ENTRY_CHUNKS
SEND_AT = END_AT + EXT // 128
POT_AT = SEND_AT + GHOSTS // 128
MISC_AT = POT_AT + NODES // 128
TABLE_CHUNKS = MISC_AT + 1


def groups_of(size, bits):
    mask = sum(bits)
    members = {}
    for i in range(size):
        members.setdefault(i & ~mask, []).append(i)
    return list(members.values())


def spread(block, axis, size, bits):
    members = groups_of(size, bits)
    copies = jnp.broadcast_to(block[None], (len(members[0]),) + block.shape)
    return lax.all_to_all(copies, axis, 0, 0, axis_index_groups=members)


def partition_table(cell_nodes, send_list, potential, cell_scale, node_count):
    shifted = jnp.where(cell_nodes >= NODES, cell_nodes - NODES, cell_nodes + GHOSTS)
    slots = jnp.pad(shifted, ((0, 0), (0, NPC_PAD - NPC))).reshape(-1)
    send = send_list.reshape(-1)
    keys = jnp.concatenate([shifted.reshape(-1), send + GHOSTS])
    tagged = keys * 4096 + lax.iota(jnp.int32, ENTRIES)
    ordered = lax.sort(tagged)
    entry = ordered & 4095
    sorted_key = ordered >> 12
    from_slot = (entry // NPC) * NPC_PAD + entry % NPC
    position = jnp.where(entry < CELLS * NPC, from_slot, entry + (CELLS * NPC_PAD - CELLS * NPC))
    position = jnp.pad(position, (0, ENTRY_PAD - ENTRIES))
    sorted_key = jnp.pad(sorted_key, (0, ENTRY_PAD - ENTRIES), constant_values=PAD_KEY)
    nodes = lax.iota(jnp.int32, EXT)
    up_to = jnp.sum((keys[None, :] <= nodes[:, None]).astype(jnp.int32), axis=1)
    before = jnp.concatenate([jnp.zeros((1,), jnp.int32), up_to[:-1]])
    end = jnp.where(up_to > before, up_to - 1, -1)
    misc = jnp.concatenate([cell_scale, node_count.astype(jnp.float32), jnp.zeros((119,), jnp.float32)])
    ints = jnp.concatenate([slots, position, sorted_key, end, send]).astype(jnp.float32)
    return jnp.concatenate([ints, potential, misc]).reshape(TABLE_CHUNKS, 128)


def chunk(c):
    return pl.ds(c * 128, 128)


def rows(g):
    return pl.ds(pl.multiple_of(g * 8, 8), 8)


def picked(sources, index):
    low = index & 127
    high = index >> 7
    total = jnp.zeros((8, 128), jnp.float32)
    for j, source in enumerate(sources):
        total = jnp.where(high == j, jnp.take_along_axis(source, low, axis=1), total)
    return total


def filter_kernel(
    coef, table, start, matrix, f_ref, g_ref,
    mat_hi, mat_lo, idx, pos, off, cont, end, send, scale, cur, prev, ext, vals, prod, arrived, w, halo, sums,
):
    lane = lax.broadcasted_iota(jnp.int32, (8, 128), 1)

    for k in range(CELL_CHUNKS):
        whole = matrix[k * 128 : (k + 1) * 128, :]
        high_part = whole.astype(jnp.bfloat16)
        low_part = (whole - high_part.astype(jnp.float32)).astype(jnp.bfloat16)
        mat_hi[k * 128 : (k + 1) * 128, :] = high_part
        mat_lo[k * 128 : (k + 1) * 128, :] = low_part

    def to_int(dest, first, count):
        def at(c, _):
            src = pl.ds(pl.multiple_of((first + c) * 128, 128), 128)
            dst = pl.ds(pl.multiple_of(c * 128, 128), 128)
            dest[:, dst] = table[:, src].astype(jnp.int32)
            return 0

        lax.fori_loop(0, count, at, 0)

    to_int(idx, IDX_AT, CELLS * CELL_CHUNKS)
    to_int(pos, POS_AT, ENTRY_CHUNKS)
    to_int(end, END_AT, EXT // 128)
    to_int(send, SEND_AT, GHOSTS // 128)
    for c in range(CELLS):
        column = table[:, MISC_AT * 128 + c : MISC_AT * 128 + c + 1]
        scale[c * 32 : (c + 1) * 32, :] = jnp.broadcast_to(column, (PARTS, 128))

    def run_of(q, _):
        here = pl.ds(pl.multiple_of((KEY_AT + q) * 128, 128), 128)
        back = pl.ds(pl.multiple_of((KEY_AT + jnp.maximum(q - 1, 0)) * 128, 128), 128)
        dst = pl.ds(pl.multiple_of(q * 128, 128), 128)
        for g in range(GROUPS):
            r = pl.ds(g * 8, 8)
            key = table[r, here]
            count = jnp.ones((8, 128), jnp.float32)
            for d in (1, 2, 4, 8, 16, 32, 64):
                same = (pltpu.roll(key, d, 1) == key) & (lane >= d)
                count = count + jnp.where(same, pltpu.roll(count, d, 1), 0.0)
            place = count.astype(jnp.int32) - 1
            off[r, dst] = place
            last = jnp.broadcast_to(table[r, back][:, 127:128], (8, 128))
            goes_on = (last == key) & (q > 0)
            cont[r, dst] = jnp.where(goes_on, 1.0, 0.0)
        return 0

    lax.fori_loop(0, ENTRY_CHUNKS, run_of, 0)
    keys = table[:, KEY_AT * 128 : (KEY_AT + ENTRY_CHUNKS) * 128]
    ghost_entries = jnp.sum(jnp.where(keys < GHOSTS, 1.0, 0.0), axis=1, keepdims=True)
    most = jnp.max(ghost_entries).astype(jnp.int32)
    least = jnp.min(ghost_entries).astype(jnp.int32)
    ghost_stop = (most + 127) // 128
    own_start = least // 128

    live = table[:, MISC_AT * 128 + 8 : MISC_AT * 128 + 9].astype(jnp.int32)
    node = lax.broadcasted_iota(jnp.int32, (PARTS, NODES), 1)
    cur[...] = jnp.where(node < live, start[...], 0.0)
    prev[...] = jnp.zeros((PARTS, NODES), jnp.float32)

    def wrap(values, k):
        c = chunk(k)
        halo[2:34, c] = values
        halo[0:2, c] = values[30:32]
        halo[34:36, c] = values[0:2]

    def into_order(first, stop, with_arrived):
        def group(g, _):
            r = rows(g)
            sources = [
                prod[pl.ds(pl.multiple_of(c * 32 + g * 8, 8), 8), chunk(k)]
                for c in range(CELLS)
                for k in range(CELL_CHUNKS)
            ]
            if with_arrived:
                sources += [arrived[r, chunk(k)] for k in range(4)]

            def at(q, _):
                here = pl.ds(pl.multiple_of(q * 128, 128), 128)
                w[r, here] = picked(sources, pos[r, here])
                return 0

            lax.fori_loop(first, stop, at, 0)
            return 0

        lax.fori_loop(0, GROUPS, group, 0)

        def along(q, carry):
            here = pl.ds(pl.multiple_of(q * 128, 128), 128)
            left = []
            for g in range(GROUPS):
                r = pl.ds(g * 8, 8)
                x = w[r, here]
                place = off[r, here]
                for d in (1, 2, 4, 8, 16, 32, 64):
                    x = x + jnp.where(place >= d, pltpu.roll(x, d, 1), 0.0)
                x = x + cont[r, here] * carry[g]
                w[r, here] = x
                left.append(jnp.broadcast_to(x[:, 127:128], (8, 128)))
            return tuple(left)

        none = jnp.zeros((8, 128), jnp.float32)
        lax.fori_loop(first, stop, along, (none,) * GROUPS)

    def run_ends(first, stop, node_first, node_count, dest):
        def group(g, _):
            r = rows(g)
            index = [end[r, chunk(node_first + n)] for n in range(node_count)]

            def at(q, totals):
                source = w[r, pl.ds(pl.multiple_of(q * 128, 128), 128)]
                return tuple(
                    jnp.where((i >> 7) == q, jnp.take_along_axis(source, i & 127, axis=1), t)
                    for i, t in zip(index, totals)
                )

            none = jnp.zeros((8, 128), jnp.float32)
            totals = lax.fori_loop(first, stop, at, (none,) * node_count)
            for n in range(node_count):
                dest[r, chunk(n)] = totals[n]
            return 0

        lax.fori_loop(0, GROUPS, group, 0)

    def step(i, _):
        def outgoing(g, _):
            r = rows(g)
            sources = [cur[r, chunk(j)] for j in range(NODES // 128)]
            for k in range(4):
                sums[r, chunk(k)] = picked(sources, send[r, chunk(k)])
            return 0

        lax.fori_loop(0, GROUPS, outgoing, 0)
        for k in range(4):
            wrap(sums[:, k * 128 : (k + 1) * 128], k)
        for k, o in enumerate(OFFSETS):
            ext[:, k * 128 : (k + 1) * 128] = halo[2 + o : 34 + o, k * 128 : (k + 1) * 128]
        ext[:, GHOSTS:] = cur[...]

        def gather(g, _):
            r = rows(g)
            sources = [ext[r, chunk(j)] for j in range(EXT // 128)]

            def cell(c, _):
                for k in range(CELL_CHUNKS):
                    here = pl.ds(pl.multiple_of(c * NPC_PAD + k * 128, 128), 128)
                    there = pl.ds(pl.multiple_of(c * 32 + g * 8, 8), 8)
                    vals[there, chunk(k)] = picked(sources, idx[r, here])
                return 0

            lax.fori_loop(0, CELLS, cell, 0)
            return 0

        lax.fori_loop(0, GROUPS, gather, 0)

        x = vals[...]
        high = x.astype(jnp.bfloat16)
        low = (x - high.astype(jnp.float32)).astype(jnp.bfloat16)

        def dot(a, b):
            return jnp.dot(a, b, preferred_element_type=jnp.float32)

        y = dot(high, mat_hi[...]) + (dot(low, mat_hi[...]) + dot(high, mat_lo[...]))
        for k in range(CELL_CHUNKS):
            prod[:, k * 128 : (k + 1) * 128] = y[:, k * 128 : (k + 1) * 128] * scale[...]

        into_order(0, ghost_stop, False)
        run_ends(0, ghost_stop, 0, 4, sums)
        for k in range(4):
            wrap(sums[:, k * 128 : (k + 1) * 128], k)
        for k, o in enumerate(OFFSETS):
            arrived[:, k * 128 : (k + 1) * 128] = halo[2 - o : 34 - o, k * 128 : (k + 1) * 128]

        into_order(own_start, ENTRY_CHUNKS, True)
        run_ends(own_start, ENTRY_CHUNKS, 4, 16, sums)

        degree = lax.rem(i, DEGREE)
        gain = coef[degree]
        back = coef[DEGREE + degree]
        centre = coef[2 * DEGREE]

        def blend(c, _):
            here = pl.ds(pl.multiple_of(c * 128, 128), 128)
            v = cur[:, here]
            pot = table[:, pl.ds(pl.multiple_of((POT_AT + c) * 128, 128), 128)]
            hv = sums[:, here] + pot * v
            before = prev[:, here]
            following = gain * (hv - centre * v)
            following = jnp.where(degree == 0, following, following - back * before)
            g_ref[:, here] = hv
            f_ref[:, here] = v
            prev[:, here] = v
            cur[:, here] = following
            return 0

        lax.fori_loop(0, NODES // 128, blend, 0)
        return 0

    lax.fori_loop(0, 2 * DEGREE + 1, step, 0)


def run_filter(coef, table, start, cell_matrix):
    padded = jnp.pad(cell_matrix, ((0, NPC_PAD - NPC), (0, NPC_PAD - NPC)))
    out = jax.ShapeDtypeStruct((PARTS, NODES), jnp.float32)
    vmem = pl.BlockSpec(memory_space=pltpu.VMEM)
    f32, i32 = jnp.float32, jnp.int32
    cells = CELLS * PARTS
    return pl.pallas_call(
        filter_kernel,
        out_shape=(out, out),
        in_specs=[pl.BlockSpec(memory_space=pltpu.SMEM)] + [vmem] * 3,
        out_specs=(vmem, vmem),
        scratch_shapes=[
            pltpu.VMEM((NPC_PAD, NPC_PAD), jnp.bfloat16),
            pltpu.VMEM((NPC_PAD, NPC_PAD), jnp.bfloat16),
            pltpu.VMEM((PARTS, CELLS * NPC_PAD), i32),
            pltpu.VMEM((PARTS, ENTRY_PAD), i32),
            pltpu.VMEM((PARTS, ENTRY_PAD), i32),
            pltpu.VMEM((PARTS, ENTRY_PAD), f32),
            pltpu.VMEM((PARTS, EXT), i32),
            pltpu.VMEM((PARTS, GHOSTS), i32),
            pltpu.VMEM((cells, 128), f32),
            pltpu.VMEM((PARTS, NODES), f32),
            pltpu.VMEM((PARTS, NODES), f32),
            pltpu.VMEM((PARTS, EXT), f32),
            pltpu.VMEM((cells, NPC_PAD), f32),
            pltpu.VMEM((cells, NPC_PAD), f32),
            pltpu.VMEM((PARTS, GHOSTS), f32),
            pltpu.VMEM((PARTS, ENTRY_PAD), f32),
            pltpu.VMEM((40, GHOSTS), f32),
            pltpu.VMEM((PARTS, NODES), f32),
        ],
        compiler_params=pltpu.CompilerParams(vmem_limit_bytes=48 * 1024 * 1024),
    )(coef, table, start, padded)


def coefficients(filter_bounds):
    lowest, wanted_top, upper = filter_bounds[0], filter_bounds[1], filter_bounds[2]
    half_width = (upper - wanted_top) / 2.0
    centre = (upper + wanted_top) / 2.0
    sigma = half_width / (lowest - centre)
    ratio = 2.0 / sigma
    gains, backs = [sigma / half_width], [jnp.zeros_like(sigma)]
    for _ in range(DEGREE - 1):
        following = 1.0 / (ratio - sigma)
        gains.append(2.0 * following / half_width)
        backs.append(sigma * following)
        sigma = following
    return jnp.stack(gains + backs + [centre, centre])


def body(vectors, potential, cell_scale, cell_matrix, cell_nodes, send_list, node_count, filter_bounds):
    own_table = partition_table(cell_nodes, send_list[0], potential, cell_scale, node_count)
    table = spread(own_table, "mesh", PARTS, (8, 16))
    table = spread(table, "mesh", PARTS, (2, 4))
    table = spread(table, "mesh", PARTS, (1,))
    table = table.transpose(2, 1, 0, 3, 4).reshape(PARTS, TABLE_CHUNKS * 128)

    start = lax.all_to_all(vectors, "mesh", 0, 0, tiled=True)
    f, g = run_filter(coefficients(filter_bounds), table, start, cell_matrix)
    filtered = lax.all_to_all(f, "mesh", 0, 0, tiled=True)
    applied = lax.all_to_all(g, "mesh", 0, 0, tiled=True)

    band_rows = filtered.shape[0]
    z_lo = groups_of(16, (1, 2))
    both = jnp.stack([filtered, applied]).reshape(2, band_rows, 4, NODES // 4)
    both = lax.all_to_all(both.transpose(2, 0, 1, 3), "band", 0, 0, axis_index_groups=z_lo)
    right = both[:, 0].reshape(4 * band_rows, NODES // 4)
    left = both[:, 1].reshape(4 * band_rows, NODES // 4)
    right = spread(right, "band", 16, (4, 8)).reshape(16 * band_rows, NODES // 4)
    partial = lax.dot_general(left, right, (((1,), (1,)), ((), ())), precision=HIGHEST)
    partial = partial.reshape(4, band_rows, 16 * band_rows)
    partial = lax.all_to_all(partial, "band", 0, 0, axis_index_groups=z_lo).sum(0)
    row = lax.all_to_all(partial, "mesh", 0, 0, tiled=True).sum(0, keepdims=True)
    row = row / (NODES * PARTS)
    hproj = lax.all_to_all(jnp.broadcast_to(row, partial.shape), "mesh", 0, 0, tiled=True)
    return filtered, hproj


def solution(mesh):
    placed = (
        P("band", "mesh"),
        P("mesh"),
        P("mesh"),
        P(),
        P("mesh", None),
        P("mesh", None, None),
        P("mesh"),
        P(),
    )
    return jax.shard_map(
        body,
        mesh=mesh,
        in_specs=placed,
        out_specs=(P("band", "mesh"), P("band", None)),
        check_vma=False,
    )
```

```python
import functools

import jax
import jax.numpy as jnp
from jax import lax
from jax.experimental import pallas as pl
from jax.experimental.pallas import tpu as pltpu
from jax.sharding import PartitionSpec as P

DEGREE = 3
OFFSETS = (-2, -1, 1, 2)
HIGHEST = lax.Precision.HIGHEST

PARTS = 32
GROUPS = PARTS // 8
NODES = 2048
SLOTS = 128
GHOSTS = 4 * SLOTS
EXT = GHOSTS + NODES
CELLS = 8
NPC = 343
NPC_PAD = 384
CELL_CHUNKS = NPC_PAD // 128
ENTRIES = CELLS * NPC + GHOSTS
ENTRY_CHUNKS = 26
ENTRY_PAD = ENTRY_CHUNKS * 128
FEW = 5
SKIP = 2
SHORT_RUN = 16

IDX_AT = 0
POS_AT = IDX_AT + CELLS * CELL_CHUNKS
PLACE_AT = POS_AT + ENTRY_CHUNKS
END_AT = PLACE_AT + ENTRY_CHUNKS
SEND_AT = END_AT + EXT // 128
POT_AT = SEND_AT + GHOSTS // 128
MISC_AT = POT_AT + NODES // 128
TABLE_CHUNKS = MISC_AT + 1


def groups_of(size, bits):
    mask = sum(bits)
    members = {}
    for i in range(size):
        members.setdefault(i & ~mask, []).append(i)
    return list(members.values())


def spread(block, axis, size, bits):
    members = groups_of(size, bits)
    copies = jnp.broadcast_to(block[None], (len(members[0]),) + block.shape)
    return lax.all_to_all(copies, axis, 0, 0, axis_index_groups=members)


def partition_table(cell_nodes, send_list, potential, cell_scale, node_count):
    shifted = jnp.where(cell_nodes >= NODES, cell_nodes - NODES, cell_nodes + GHOSTS)
    slots = jnp.pad(shifted, ((0, 0), (0, NPC_PAD - NPC))).reshape(-1)
    send = send_list.reshape(-1)
    keys = jnp.concatenate([shifted.reshape(-1), send + GHOSTS])
    tagged = keys * 4096 + lax.iota(jnp.int32, ENTRIES)
    ordered = lax.sort(tagged)
    entry = ordered & 4095
    sorted_key = ordered >> 12
    from_slot = (entry // NPC) * NPC_PAD + entry % NPC
    position = jnp.where(entry < CELLS * NPC, from_slot, entry + (CELLS * NPC_PAD - CELLS * NPC))
    nodes = lax.iota(jnp.int32, EXT)
    up_to = jnp.sum((keys[None, :] <= nodes[:, None]).astype(jnp.int32), axis=1)
    before = jnp.concatenate([jnp.zeros((1,), jnp.int32), up_to[:-1]])
    end = jnp.where(up_to > before, up_to - 1, -1)
    first = jnp.sum((keys[None, :] < sorted_key[:, None]).astype(jnp.int32), axis=1)
    place = lax.iota(jnp.int32, ENTRIES) - first
    longest = jnp.max(place) + 1
    ghost_entries = up_to[GHOSTS - 1]
    place = jnp.pad(place, (0, ENTRY_PAD - ENTRIES))
    position = jnp.pad(position, (0, ENTRY_PAD - ENTRIES))
    misc = jnp.concatenate([
        cell_scale,
        jnp.stack([node_count[0], ghost_entries, longest]).astype(jnp.float32),
        jnp.zeros((117,), jnp.float32),
    ])
    ints = jnp.concatenate([slots, position, place, end, send]).astype(jnp.float32)
    return jnp.concatenate([ints, potential, misc]).reshape(TABLE_CHUNKS, 128)


def chunk(c):
    return pl.ds(c * 128, 128)


def rows(g):
    return pl.ds(pl.multiple_of(g * 8, 8), 8)


def picked(sources, index):
    low = index & 127
    high = index >> 7
    total = jnp.zeros((8, 128), jnp.float32)
    for j, source in sources:
        total = jnp.where(high == j, jnp.take_along_axis(source, low, axis=1), total)
    return total


def filter_kernel(
    step_count, last, coef, table, start, matrix, out,
    mat_hi, mat_lo, idx, pos, place, end, send, scale, cur, prev, ext, vals, prod, arrived, w, halo, sums,
):
    lane = lax.broadcasted_iota(jnp.int32, (8, 128), 1)
    last_lane = jnp.full((8, 128), 127, jnp.int32)

    for k in range(CELL_CHUNKS):
        whole = matrix[k * 128 : (k + 1) * 128, :]
        high_part = whole.astype(jnp.bfloat16)
        low_part = (whole - high_part.astype(jnp.float32)).astype(jnp.bfloat16)
        mat_hi[k * 128 : (k + 1) * 128, :] = high_part
        mat_lo[k * 128 : (k + 1) * 128, :] = low_part

    def to_int(dest, first, count):
        for c in range(count):
            dest[:, chunk(c)] = table[:, chunk(first + c)].astype(jnp.int32)

    to_int(idx, IDX_AT, CELLS * CELL_CHUNKS)
    to_int(pos, POS_AT, ENTRY_CHUNKS)
    to_int(place, PLACE_AT, ENTRY_CHUNKS)
    to_int(end, END_AT, EXT // 128)
    to_int(send, SEND_AT, GHOSTS // 128)
    for c in range(CELLS):
        column = table[:, MISC_AT * 128 + c : MISC_AT * 128 + c + 1]
        scale[c * 32 : (c + 1) * 32, :] = jnp.broadcast_to(column, (PARTS, 128))

    def misc(c):
        return table[:, MISC_AT * 128 + CELLS + c : MISC_AT * 128 + CELLS + c + 1]

    few = (jnp.max(misc(1)).astype(jnp.int32) <= FEW * 128) & (jnp.min(misc(1)).astype(jnp.int32) >= SKIP * 128)
    long_runs = jnp.max(misc(2)).astype(jnp.int32) > SHORT_RUN

    if last:
        cur[...] = start[...]
    else:
        live = misc(0).astype(jnp.int32)
        node = lax.broadcasted_iota(jnp.int32, (PARTS, NODES), 1)
        cur[...] = jnp.where(node < live, start[...], 0.0)
        prev[...] = jnp.zeros((PARTS, NODES), jnp.float32)

    def over_groups(body):
        def at(g, _):
            body(g, rows(g))
            return 0

        lax.fori_loop(0, GROUPS, at, 0)

    def wrap(values, k):
        c = chunk(k)
        halo[2:34, c] = values
        halo[0:2, c] = values[30:32]
        halo[34:36, c] = values[0:2]

    def products_of(g):
        return [
            (c * CELL_CHUNKS + k, prod[pl.ds(pl.multiple_of(c * 32 + g * 8, 8), 8), chunk(k)])
            for c in range(CELLS)
            for k in range(CELL_CHUNKS)
        ]

    def pick_into_w(r, sources, first, stop):
        for q in range(first, stop):
            w[r, chunk(q)] = picked(sources, pos[r, chunk(q)])

    def doubling(r, stop, distances):
        for d in distances:
            back = (lane - d) & 127
            for q in range(stop):
                x = w[r, chunk(q)]
                near = jnp.minimum(place[r, chunk(q)], lane) >= d
                w[r, chunk(q)] = x + jnp.where(near, jnp.take_along_axis(x, back, axis=1), 0.0)

    def run_sums(r, stop):
        xs = [w[r, chunk(q)] for q in range(stop)]
        at = [jnp.minimum(place[r, chunk(q)], lane) for q in range(stop)]
        d = 1
        while d < SHORT_RUN:
            back = (lane - d) & 127
            moved = [jnp.take_along_axis(x, back, axis=1) for x in xs]
            xs = [x + jnp.where(a >= d, m, 0.0) for x, a, m in zip(xs, at, moved)]
            d *= 2
        for q in range(stop):
            w[r, chunk(q)] = xs[q]

        @pl.when(long_runs)
        def _():
            doubling(r, stop, (16, 32, 64))

        carry = jnp.zeros((8, 128), jnp.float32)
        for q in range(stop):
            x = w[r, chunk(q)]
            total = jnp.take_along_axis(x, last_lane, axis=1)
            goes_on = place[r, chunk(q)] > lane
            through = jnp.take_along_axis(jnp.where(goes_on, 1.0, 0.0), last_lane, axis=1)
            w[r, chunk(q)] = x + jnp.where(goes_on, carry, 0.0)
            carry = total + through * carry

    def run_ends(r, first, stop, node_first, node_count, dest):
        sources = [(q, w[r, chunk(q)]) for q in range(first, stop)]
        for n in range(node_count):
            dest[r, chunk(n)] = picked(sources, end[r, chunk(node_first + n)])

    def ghost_sums(stop):
        def picks(g, r):
            pick_into_w(r, products_of(g), 0, stop)
            run_sums(r, stop)
            run_ends(r, 0, stop, 0, 4, sums)

        over_groups(picks)

    def own_sums(first):
        def picks(g, r):
            sources = products_of(g)
            base = CELLS * CELL_CHUNKS
            sources += [(base + k, arrived[r, chunk(k)]) for k in range(4)]
            pick_into_w(r, sources, first, ENTRY_CHUNKS)

        over_groups(picks)
        over_groups(lambda g, r: run_sums(r, ENTRY_CHUNKS))
        over_groups(lambda g, r: run_ends(r, first, ENTRY_CHUNKS, 4, 16, sums))

    def apply():
        def outgoing(g, r):
            sources = [(j, cur[r, chunk(j)]) for j in range(NODES // 128)]
            for k in range(4):
                sums[r, chunk(k)] = picked(sources, send[r, chunk(k)])

        over_groups(outgoing)
        for k in range(4):
            wrap(sums[:, k * 128 : (k + 1) * 128], k)
        for k, o in enumerate(OFFSETS):
            ext[:, k * 128 : (k + 1) * 128] = halo[2 + o : 34 + o, k * 128 : (k + 1) * 128]
        ext[:, GHOSTS:] = cur[...]

        def gather(g, r):
            sources = [(j, ext[r, chunk(j)]) for j in range(EXT // 128)]

            def some_cells(b, _):
                for u in range(4):
                    c = b * 4 + u
                    for k in range(CELL_CHUNKS):
                        here = pl.ds(pl.multiple_of(c * NPC_PAD + k * 128, 128), 128)
                        there = pl.ds(pl.multiple_of(c * 32 + g * 8, 8), 8)
                        vals[there, chunk(k)] = picked(sources, idx[r, here])
                return 0

            lax.fori_loop(0, 2, some_cells, 0)

        over_groups(gather)

        x = vals[...]
        high = x.astype(jnp.bfloat16)
        low = (x - high.astype(jnp.float32)).astype(jnp.bfloat16)

        def dot(a, b):
            return jnp.dot(a, b, preferred_element_type=jnp.float32)

        y = dot(high, mat_hi[...]) + (dot(low, mat_hi[...]) + dot(high, mat_lo[...]))
        for k in range(CELL_CHUNKS):
            prod[:, k * 128 : (k + 1) * 128] = y[:, k * 128 : (k + 1) * 128] * scale[...]

        pl.when(few)(lambda: ghost_sums(FEW))
        pl.when(~few)(lambda: ghost_sums(ENTRY_CHUNKS))
        for k in range(4):
            wrap(sums[:, k * 128 : (k + 1) * 128], k)
        for k, o in enumerate(OFFSETS):
            arrived[:, k * 128 : (k + 1) * 128] = halo[2 - o : 34 - o, k * 128 : (k + 1) * 128]

        pl.when(few)(lambda: own_sums(SKIP))
        pl.when(~few)(lambda: own_sums(0))

    def step(i, _):
        apply()
        degree = lax.rem(i, DEGREE)
        gain = coef[degree]
        back = coef[DEGREE + degree]
        centre = coef[2 * DEGREE]
        for c in range(NODES // 128):
            here = chunk(c)
            v = cur[:, here]
            hv = sums[:, here] + table[:, chunk(POT_AT + c)] * v
            following = gain * (hv - centre * v)
            following = jnp.where(degree == 0, following, following - back * prev[:, here])
            prev[:, here] = v
            cur[:, here] = following
        return 0

    if last:
        apply()
        for c in range(NODES // 128):
            out[:, chunk(c)] = sums[:, chunk(c)] + table[:, chunk(POT_AT + c)] * cur[:, chunk(c)]
    else:
        lax.fori_loop(0, step_count, step, 0)
        out[...] = cur[...]


def run_filter(coef, table, start, cell_matrix, step_count, last):
    padded = jnp.pad(cell_matrix, ((0, NPC_PAD - NPC), (0, NPC_PAD - NPC)))
    vmem = pl.BlockSpec(memory_space=pltpu.VMEM)
    f32, i32 = jnp.float32, jnp.int32
    cells = CELLS * PARTS
    return pl.pallas_call(
        functools.partial(filter_kernel, step_count, last),
        out_shape=jax.ShapeDtypeStruct((PARTS, NODES), f32),
        in_specs=[pl.BlockSpec(memory_space=pltpu.SMEM)] + [vmem] * 3,
        out_specs=vmem,
        scratch_shapes=[
            pltpu.VMEM((NPC_PAD, NPC_PAD), jnp.bfloat16),
            pltpu.VMEM((NPC_PAD, NPC_PAD), jnp.bfloat16),
            pltpu.VMEM((PARTS, CELLS * NPC_PAD), i32),
            pltpu.VMEM((PARTS, ENTRY_PAD), i32),
            pltpu.VMEM((PARTS, ENTRY_PAD), i32),
            pltpu.VMEM((PARTS, EXT), i32),
            pltpu.VMEM((PARTS, GHOSTS), i32),
            pltpu.VMEM((cells, 128), f32),
            pltpu.VMEM((PARTS, NODES), f32),
            pltpu.VMEM((PARTS, NODES), f32),
            pltpu.VMEM((PARTS, EXT), f32),
            pltpu.VMEM((cells, NPC_PAD), f32),
            pltpu.VMEM((cells, NPC_PAD), f32),
            pltpu.VMEM((PARTS, GHOSTS), f32),
            pltpu.VMEM((PARTS, ENTRY_PAD), f32),
            pltpu.VMEM((40, GHOSTS), f32),
            pltpu.VMEM((PARTS, NODES), f32),
        ],
        compiler_params=pltpu.CompilerParams(vmem_limit_bytes=48 * 1024 * 1024),
    )(coef, table, start, padded)


def coefficients(filter_bounds):
    lowest, wanted_top, upper = filter_bounds[0], filter_bounds[1], filter_bounds[2]
    half_width = (upper - wanted_top) / 2.0
    centre = (upper + wanted_top) / 2.0
    sigma = half_width / (lowest - centre)
    ratio = 2.0 / sigma
    gains, backs = [sigma / half_width], [jnp.zeros_like(sigma)]
    for _ in range(DEGREE - 1):
        following = 1.0 / (ratio - sigma)
        gains.append(2.0 * following / half_width)
        backs.append(sigma * following)
        sigma = following
    return jnp.stack(gains + backs + [centre, centre])


def body(vectors, potential, cell_scale, cell_matrix, cell_nodes, send_list, node_count, filter_bounds):
    own_table = partition_table(cell_nodes, send_list[0], potential, cell_scale, node_count)
    table = spread(own_table, "mesh", PARTS, (8, 16))
    table = spread(table, "mesh", PARTS, (2, 4))
    table = spread(table, "mesh", PARTS, (1,))
    table = table.transpose(2, 1, 0, 3, 4).reshape(PARTS, TABLE_CHUNKS * 128)

    start = lax.all_to_all(vectors, "mesh", 0, 0, tiled=True)
    coef = coefficients(filter_bounds)
    f = run_filter(coef, table, start, cell_matrix, 2 * DEGREE, False)
    g = run_filter(coef, table, f, cell_matrix, 1, True)
    filtered = lax.all_to_all(f, "mesh", 0, 0, tiled=True)
    applied = lax.all_to_all(g, "mesh", 0, 0, tiled=True)

    band_rows = filtered.shape[0]
    z_lo = groups_of(16, (1, 2))
    both = jnp.stack([filtered, applied]).reshape(2, band_rows, 4, NODES // 4)
    both = lax.all_to_all(both.transpose(2, 0, 1, 3), "band", 0, 0, axis_index_groups=z_lo)
    right = both[:, 0].reshape(4 * band_rows, NODES // 4)
    left = both[:, 1].reshape(4 * band_rows, NODES // 4)
    right = spread(right, "band", 16, (4, 8)).reshape(16 * band_rows, NODES // 4)
    partial = lax.dot_general(left, right, (((1,), (1,)), ((), ())), precision=HIGHEST)
    partial = partial.reshape(4, band_rows, 16 * band_rows)
    partial = lax.all_to_all(partial, "band", 0, 0, axis_index_groups=z_lo).sum(0)
    row = lax.all_to_all(partial, "mesh", 0, 0, tiled=True).sum(0, keepdims=True)
    row = row / (NODES * PARTS)
    hproj = lax.all_to_all(jnp.broadcast_to(row, partial.shape), "mesh", 0, 0, tiled=True)
    return filtered, hproj


def solution(mesh):
    placed = (
        P("band", "mesh"),
        P("mesh"),
        P("mesh"),
        P(),
        P("mesh", None),
        P("mesh", None, None),
        P("mesh"),
        P(),
    )
    return jax.shard_map(
        body,
        mesh=mesh,
        in_specs=placed,
        out_specs=(P("band", "mesh"), P("band", None)),
        check_vma=False,
    )
```

```python
import functools

import jax
import jax.numpy as jnp
from jax import lax
from jax.experimental import pallas as pl
from jax.experimental.pallas import tpu as pltpu
from jax.sharding import PartitionSpec as P

DEGREE = 3
OFFSETS = (-2, -1, 1, 2)
HIGHEST = lax.Precision.HIGHEST

PARTS = 32
GROUPS = PARTS // 8
NODES = 2048
SLOTS = 128
GHOSTS = 4 * SLOTS
EXT = GHOSTS + NODES
CELLS = 8
NPC = 343
NPC_PAD = 384
CELL_CHUNKS = NPC_PAD // 128
ENTRIES = CELLS * NPC + GHOSTS
ENTRY_CHUNKS = 26
ENTRY_PAD = ENTRY_CHUNKS * 128
FEW = 5
SKIP = 3
SHORT_RUN = 16

IDX_AT = 0
POS_AT = IDX_AT + CELLS * CELL_CHUNKS
PLACE_AT = POS_AT + ENTRY_CHUNKS
END_AT = PLACE_AT + ENTRY_CHUNKS
SEND_AT = END_AT + EXT // 128
POT_AT = SEND_AT + GHOSTS // 128
MISC_AT = POT_AT + NODES // 128
TABLE_CHUNKS = MISC_AT + 1


def groups_of(size, bits):
    mask = sum(bits)
    members = {}
    for i in range(size):
        members.setdefault(i & ~mask, []).append(i)
    return list(members.values())


def spread(block, axis, size, bits):
    members = groups_of(size, bits)
    copies = jnp.broadcast_to(block[None], (len(members[0]),) + block.shape)
    return lax.all_to_all(copies, axis, 0, 0, axis_index_groups=members)


def swapped(block, axis, size, distance):
    return lax.ppermute(block, axis, [(i ^ distance, i) for i in range(size)])


def in_place(own, received, mine):
    blocks = [own, *received]
    return jnp.stack([lax.select_n(mine, *[blocks[j ^ m] for m in range(4)]) for j in range(4)])


def exchange(pieces, axis, size, unit):
    mine = (lax.axis_index(axis) // unit) % 4
    kept, *sent = [lax.dynamic_index_in_dim(pieces, mine ^ d, 0, keepdims=False) for d in range(4)]
    return in_place(kept, [swapped(p, axis, size, (d + 1) * unit) for d, p in enumerate(sent)], mine)


def collected(block, axis, size, unit):
    mine = (lax.axis_index(axis) // unit) % 4
    return in_place(block, [swapped(block, axis, size, d * unit) for d in (1, 2, 3)], mine)


def partition_table(cell_nodes, send_list, potential, cell_scale, node_count):
    shifted = jnp.where(cell_nodes >= NODES, cell_nodes - NODES, cell_nodes + GHOSTS)
    slots = jnp.pad(shifted, ((0, 0), (0, NPC_PAD - NPC))).reshape(-1)
    send = send_list.reshape(-1)
    keys = jnp.concatenate([shifted.reshape(-1), send + GHOSTS])
    tagged = keys * 4096 + lax.iota(jnp.int32, ENTRIES)
    ordered = lax.sort(tagged)
    entry = ordered & 4095
    sorted_key = ordered >> 12
    from_slot = (entry // NPC) * NPC_PAD + entry % NPC
    position = jnp.where(entry < CELLS * NPC, from_slot, entry + (CELLS * NPC_PAD - CELLS * NPC))
    nodes = lax.iota(jnp.int32, EXT)
    up_to = jnp.sum((keys[None, :] <= nodes[:, None]).astype(jnp.int32), axis=1)
    before = jnp.concatenate([jnp.zeros((1,), jnp.int32), up_to[:-1]])
    end = jnp.where(up_to > before, up_to - 1, -1)
    first = jnp.sum((keys[None, :] < sorted_key[:, None]).astype(jnp.int32), axis=1)
    place = lax.iota(jnp.int32, ENTRIES) - first
    longest = jnp.max(place) + 1
    ghost_entries = up_to[GHOSTS - 1]
    place = jnp.pad(place, (0, ENTRY_PAD - ENTRIES))
    position = jnp.pad(position, (0, ENTRY_PAD - ENTRIES))
    misc = jnp.concatenate([
        cell_scale,
        jnp.stack([node_count[0], ghost_entries, longest]).astype(jnp.float32),
        jnp.zeros((117,), jnp.float32),
    ])
    ints = jnp.concatenate([slots, position, place, end, send]).astype(jnp.float32)
    return jnp.concatenate([ints, potential, misc]).reshape(TABLE_CHUNKS, 128)


def chunk(c):
    return pl.ds(c * 128, 128)


def rows(g):
    return pl.ds(pl.multiple_of(g * 8, 8), 8)


def picked(sources, index):
    low = index & 127
    high = index >> 7
    total = jnp.zeros((8, 128), jnp.float32)
    for j, source in sources:
        total = jnp.where(high == j, jnp.take_along_axis(source, low, axis=1), total)
    return total


def filter_kernel(
    step_count, last, coef, table, start, matrix, out,
    mat_hi, mat_lo, idx, pos, place, end, send, scale, cur, prev, ext, vals, prod, arrived, w, halo, sums,
):
    lane = lax.broadcasted_iota(jnp.int32, (8, 128), 1)
    last_lane = jnp.full((8, 128), 127, jnp.int32)

    for k in range(CELL_CHUNKS):
        whole = matrix[k * 128 : (k + 1) * 128, :]
        high_part = whole.astype(jnp.bfloat16)
        low_part = (whole - high_part.astype(jnp.float32)).astype(jnp.bfloat16)
        mat_hi[k * 128 : (k + 1) * 128, :] = high_part
        mat_lo[k * 128 : (k + 1) * 128, :] = low_part

    def to_int(dest, first, count):
        for c in range(count):
            dest[:, chunk(c)] = table[:, chunk(first + c)].astype(jnp.int32)

    to_int(idx, IDX_AT, CELLS * CELL_CHUNKS)
    to_int(pos, POS_AT, ENTRY_CHUNKS)
    to_int(place, PLACE_AT, ENTRY_CHUNKS)
    to_int(end, END_AT, EXT // 128)
    to_int(send, SEND_AT, GHOSTS // 128)
    for c in range(CELLS):
        column = table[:, MISC_AT * 128 + c : MISC_AT * 128 + c + 1]
        scale[c * 32 : (c + 1) * 32, :] = jnp.broadcast_to(column, (PARTS, 128))

    def misc(c):
        return table[:, MISC_AT * 128 + CELLS + c : MISC_AT * 128 + CELLS + c + 1]

    short = jnp.max(misc(1)).astype(jnp.int32) <= FEW * 128
    short &= jnp.min(misc(1)).astype(jnp.int32) >= SKIP * 128
    short &= jnp.max(misc(2)).astype(jnp.int32) <= SHORT_RUN

    quarter = NODES // 4
    if last:
        for q in range(4):
            cur[:, q * quarter : (q + 1) * quarter] = start[q * 32 : (q + 1) * 32, :]
    else:
        live = misc(0).astype(jnp.int32)
        node = lax.broadcasted_iota(jnp.int32, (PARTS, NODES), 1)
        cur[...] = jnp.where(node < live, start[...], 0.0)
        prev[...] = jnp.zeros((PARTS, NODES), jnp.float32)

    def over_groups(body):
        def at(g, _):
            body(g, rows(g))
            return 0

        lax.fori_loop(0, GROUPS, at, 0)

    def wrap(values, k):
        c = chunk(k)
        halo[2:34, c] = values
        halo[0:2, c] = values[30:32]
        halo[34:36, c] = values[0:2]

    def products_of(g):
        return [
            (c * CELL_CHUNKS + k, prod[pl.ds(pl.multiple_of(c * 32 + g * 8, 8), 8), chunk(k)])
            for c in range(CELLS)
            for k in range(CELL_CHUNKS)
        ]

    def into_order(r, sources, first, stop):
        for q in range(first, stop):
            w[r, chunk(q)] = picked(sources, pos[r, chunk(q)])

    def partial_runs(places, longest):
        xs = [w[r, chunk(q)] for r, q in places]
        near = [jnp.minimum(place[r, chunk(q)], lane) for r, q in places]
        for d in [1 << k for k in range(7) if (1 << k) < longest]:
            back = (lane - d) & 127
            moved = [jnp.take_along_axis(x, back, axis=1) for x in xs]
            xs = [x + jnp.where(a >= d, m, 0.0) for x, a, m in zip(xs, near, moved)]
        for (r, q), x in zip(places, xs):
            w[r, chunk(q)] = x

    def joined_runs(r, first, stop):
        xs = [w[r, chunk(q)] for q in range(first, stop)]
        done = [(first, xs[0])]
        for q, x, before in zip(range(first + 1, stop), xs[1:], xs):
            carry = jnp.take_along_axis(before, last_lane, axis=1)
            done.append((q, x + jnp.where(place[r, chunk(q)] > lane, carry, 0.0)))
        return done

    def chained_runs(r):
        carry = jnp.zeros((8, 128), jnp.float32)
        done = []
        for q in range(ENTRY_CHUNKS):
            x = w[r, chunk(q)]
            total = jnp.take_along_axis(x, last_lane, axis=1)
            goes_on = place[r, chunk(q)] > lane
            through = jnp.take_along_axis(jnp.where(goes_on, 1.0, 0.0), last_lane, axis=1)
            done.append((q, x + jnp.where(goes_on, carry, 0.0)))
            carry = total + through * carry
        return done

    def run_ends(r, sources, node_first, node_count):
        for n in range(node_count):
            sums[r, chunk(n)] = picked(sources, end[r, chunk(node_first + n)])

    def with_arrivals(g, r):
        base = CELLS * CELL_CHUNKS
        return products_of(g) + [(base + k, arrived[r, chunk(k)]) for k in range(4)]

    fixed = [pl.ds(g * 8, 8) for g in range(GROUPS)]

    def in_order_and_summed(sources_of):
        def at(g, r):
            into_order(r, sources_of(g, r), 0, ENTRY_CHUNKS)
            partial_runs([(r, q) for q in range(ENTRY_CHUNKS)], 128)

        over_groups(at)

    def ghost_sums():
        for g, r in enumerate(fixed):
            into_order(r, products_of(g), 0, FEW)
        partial_runs([(r, q) for r in fixed for q in range(FEW)], SHORT_RUN)
        for r in fixed:
            run_ends(r, joined_runs(r, 0, FEW), 0, 4)

    def ghost_sums_any():
        in_order_and_summed(lambda g, r: products_of(g))
        over_groups(lambda g, r: run_ends(r, chained_runs(r), 0, 4))

    def own_sums():
        over_groups(lambda g, r: into_order(r, with_arrivals(g, r), SKIP, ENTRY_CHUNKS))
        for r in fixed:
            partial_runs([(r, q) for q in range(SKIP, ENTRY_CHUNKS)], SHORT_RUN)
        over_groups(lambda g, r: run_ends(r, joined_runs(r, SKIP, ENTRY_CHUNKS), 4, 16))

    def own_sums_any():
        in_order_and_summed(with_arrivals)
        over_groups(lambda g, r: run_ends(r, chained_runs(r), 4, 16))

    def apply():
        def outgoing(g, r):
            sources = [(j, cur[r, chunk(j)]) for j in range(NODES // 128)]
            for k in range(4):
                sums[r, chunk(k)] = picked(sources, send[r, chunk(k)])

        for g in range(GROUPS):
            outgoing(g, pl.ds(g * 8, 8))
        for k in range(4):
            wrap(sums[:, k * 128 : (k + 1) * 128], k)
        for k, o in enumerate(OFFSETS):
            ext[:, k * 128 : (k + 1) * 128] = halo[2 + o : 34 + o, k * 128 : (k + 1) * 128]
        ext[:, GHOSTS:] = cur[...]

        def gather(g, r):
            sources = [(j, ext[r, chunk(j)]) for j in range(EXT // 128)]

            for c in range(CELLS):
                there = pl.ds(pl.multiple_of(c * 32 + g * 8, 8), 8)
                for k in range(CELL_CHUNKS):
                    vals[there, chunk(k)] = picked(sources, idx[r, chunk(c * CELL_CHUNKS + k)])

        over_groups(gather)

        x = vals[...]
        high = x.astype(jnp.bfloat16)
        low = (x - high.astype(jnp.float32)).astype(jnp.bfloat16)

        def dot(a, b):
            return jnp.dot(a, b, preferred_element_type=jnp.float32)

        y = dot(high, mat_hi[...]) + (dot(low, mat_hi[...]) + dot(high, mat_lo[...]))
        for k in range(CELL_CHUNKS):
            prod[:, k * 128 : (k + 1) * 128] = y[:, k * 128 : (k + 1) * 128] * scale[...]

        pl.when(short)(ghost_sums)
        pl.when(~short)(ghost_sums_any)
        for k in range(4):
            wrap(sums[:, k * 128 : (k + 1) * 128], k)
        for k, o in enumerate(OFFSETS):
            arrived[:, k * 128 : (k + 1) * 128] = halo[2 - o : 34 - o, k * 128 : (k + 1) * 128]

        pl.when(short)(own_sums)
        pl.when(~short)(own_sums_any)

    def step(i, _):
        apply()
        degree = lax.rem(i, DEGREE)
        gain = coef[degree]
        back = coef[DEGREE + degree]
        centre = coef[2 * DEGREE]
        for c in range(NODES // 128):
            here = chunk(c)
            v = cur[:, here]
            hv = sums[:, here] + table[:, chunk(POT_AT + c)] * v
            following = gain * (hv - centre * v)
            following = jnp.where(degree == 0, following, following - back * prev[:, here])
            prev[:, here] = v
            cur[:, here] = following
        return 0

    if last:
        apply()
        for c in range(NODES // 128):
            cur[:, chunk(c)] = sums[:, chunk(c)] + table[:, chunk(POT_AT + c)] * cur[:, chunk(c)]
    else:
        lax.fori_loop(0, step_count, step, 0)
    for q in range(4):
        out[q * 32 : (q + 1) * 32, :] = cur[:, q * quarter : (q + 1) * quarter]


def run_filter(coef, table, start, cell_matrix, step_count, last):
    padded = jnp.pad(cell_matrix, ((0, NPC_PAD - NPC), (0, NPC_PAD - NPC)))
    vmem = pl.BlockSpec(memory_space=pltpu.VMEM)
    f32, i32 = jnp.float32, jnp.int32
    cells = CELLS * PARTS
    return pl.pallas_call(
        functools.partial(filter_kernel, step_count, last),
        out_shape=jax.ShapeDtypeStruct((4 * PARTS, NODES // 4), f32),
        in_specs=[pl.BlockSpec(memory_space=pltpu.SMEM)] + [vmem] * 3,
        out_specs=vmem,
        scratch_shapes=[
            pltpu.VMEM((NPC_PAD, NPC_PAD), jnp.bfloat16),
            pltpu.VMEM((NPC_PAD, NPC_PAD), jnp.bfloat16),
            pltpu.VMEM((PARTS, CELLS * NPC_PAD), i32),
            pltpu.VMEM((PARTS, ENTRY_PAD), i32),
            pltpu.VMEM((PARTS, ENTRY_PAD), i32),
            pltpu.VMEM((PARTS, EXT), i32),
            pltpu.VMEM((PARTS, GHOSTS), i32),
            pltpu.VMEM((cells, 128), f32),
            pltpu.VMEM((PARTS, NODES), f32),
            pltpu.VMEM((PARTS, NODES), f32),
            pltpu.VMEM((PARTS, EXT), f32),
            pltpu.VMEM((cells, NPC_PAD), f32),
            pltpu.VMEM((cells, NPC_PAD), f32),
            pltpu.VMEM((PARTS, GHOSTS), f32),
            pltpu.VMEM((PARTS, ENTRY_PAD), f32),
            pltpu.VMEM((40, GHOSTS), f32),
            pltpu.VMEM((PARTS, NODES), f32),
        ],
        compiler_params=pltpu.CompilerParams(vmem_limit_bytes=48 * 1024 * 1024),
        cost_estimate=pl.CostEstimate(
            flops=step_count * 15_000_000_000, bytes_accessed=step_count * 50_000_000, transcendentals=0
        ),
    )(coef, table, start, padded)


def coefficients(filter_bounds):
    lowest, wanted_top, upper = filter_bounds[0], filter_bounds[1], filter_bounds[2]
    half_width = (upper - wanted_top) / 2.0
    centre = (upper + wanted_top) / 2.0
    sigma = half_width / (lowest - centre)
    ratio = 2.0 / sigma
    gains, backs = [sigma / half_width], [jnp.zeros_like(sigma)]
    for _ in range(DEGREE - 1):
        following = 1.0 / (ratio - sigma)
        gains.append(2.0 * following / half_width)
        backs.append(sigma * following)
        sigma = following
    return jnp.stack(gains + backs + [centre, centre])


def body(vectors, potential, cell_scale, cell_matrix, cell_nodes, send_list, node_count, filter_bounds):
    start = lax.all_to_all(vectors, "mesh", 0, 0, tiled=True)
    own_table = partition_table(cell_nodes, send_list[0], potential, cell_scale, node_count)
    own_table, start = lax.optimization_barrier((own_table, start))
    table = collected(own_table, "mesh", PARTS, 8)
    table = spread(table, "mesh", PARTS, (2, 4))
    table = spread(table, "mesh", PARTS, (1,))
    table = table.transpose(2, 1, 0, 3, 4).reshape(PARTS, TABLE_CHUNKS * 128)

    coef = coefficients(filter_bounds)
    quarters = groups_of(16 * PARTS, (1, 2, 4, 8, 16, PARTS, 2 * PARTS))

    def to_quarters(field):
        pieces = field.reshape(4 * PARTS, NODES // 512, 128)
        pieces = lax.all_to_all(pieces, ("band", "mesh"), 0, 0, axis_index_groups=quarters)
        return pieces.reshape(4 * PARTS, NODES // 4)

    f = run_filter(coef, table, start, cell_matrix, 2 * DEGREE, False)
    f_quarter = to_quarters(f)
    g = run_filter(coef, table, f, cell_matrix, 1, True)
    left = to_quarters(g)
    band_rows = vectors.shape[0]
    filtered = exchange(f_quarter.reshape(4, band_rows, NODES // 4), "band", 16, 1)
    filtered = filtered.transpose(1, 0, 2).reshape(band_rows, NODES)

    right = collected(f_quarter, "band", 16, 4).reshape(16 * band_rows, NODES // 4)
    partial = lax.dot_general(left, right, (((1,), (1,)), ((), ())), precision=HIGHEST)

    plane = groups_of(PARTS, (1, 2, 4))
    partial = partial.reshape(4, 8, band_rows // 8, 16 * band_rows).transpose(1, 0, 2, 3)
    partial = lax.all_to_all(partial, "mesh", 0, 0, axis_index_groups=plane).sum(0)
    along_z = groups_of(16 * PARTS, (8, 16, PARTS, 2 * PARTS))
    partial = jnp.broadcast_to(partial[:, None], (4, 4) + partial.shape[1:])
    partial = partial.reshape((16,) + partial.shape[2:])
    block = lax.all_to_all(partial, ("band", "mesh"), 0, 0, axis_index_groups=along_z).sum(0)
    block = block / (NODES * PARTS)
    hproj = spread(block, "mesh", PARTS, (1, 2, 4)).reshape(band_rows, 16 * band_rows)
    return filtered, hproj


def solution(mesh):
    placed = (
        P("band", "mesh"),
        P("mesh"),
        P("mesh"),
        P(),
        P("mesh", None),
        P("mesh", None, None),
        P("mesh"),
        P(),
    )
    return jax.shard_map(
        body,
        mesh=mesh,
        in_specs=placed,
        out_specs=(P("band", "mesh"), P("band", None)),
        check_vma=False,
    )
```

```python
import functools

import jax
import jax.numpy as jnp
from jax import lax
from jax.experimental import pallas as pl
from jax.experimental.pallas import tpu as pltpu
from jax.sharding import PartitionSpec as P

DEGREE = 3
OFFSETS = (-2, -1, 1, 2)
HIGHEST = lax.Precision.HIGHEST

PARTS = 32
GROUPS = PARTS // 8
NODES = 2048
SLOTS = 128
GHOSTS = 4 * SLOTS
EXT = GHOSTS + NODES
CELLS = 8
NPC = 343
NPC_PAD = 384
CELL_CHUNKS = NPC_PAD // 128
ENTRIES = CELLS * NPC + GHOSTS
ENTRY_CHUNKS = 26
ENTRY_PAD = ENTRY_CHUNKS * 128
PAD_NODE = 4095
CELL_MULTIPLIER, CELL_SHIFT = 6115, 21
FEW = 5
SKIP = 3
SHORT_RUN = 16
WINDOWS = (
    (3, 8), (4, 11), (6, 13), (7, 16), (8, 19), (10, 21), (11, 24), (12, 26),
    (13, 26), (15, 26), (16, 26), (18, 26), (19, 26), (20, 26), (22, 26), (23, 26),
)

IDX_AT = 0
POS_AT = IDX_AT + CELLS * CELL_CHUNKS
PLACE_AT = POS_AT + ENTRY_CHUNKS
END_AT = PLACE_AT + ENTRY_CHUNKS
SEND_AT = END_AT + EXT // 128
POT_AT = SEND_AT + GHOSTS // 128
MISC_AT = POT_AT + NODES // 128
START_AT = MISC_AT + 4
TABLE_CHUNKS = START_AT + NODES // 128


def groups_of(size, bits):
    mask = sum(bits)
    members = {}
    for i in range(size):
        members.setdefault(i & ~mask, []).append(i)
    return list(members.values())


def spread(block, axis, size, bits):
    members = groups_of(size, bits)
    copies = jnp.broadcast_to(block[None], (len(members[0]),) + block.shape)
    return lax.all_to_all(copies, axis, 0, 0, axis_index_groups=members)


def swapped(block, axis, size, distance):
    return lax.ppermute(block, axis, [(i ^ distance, i) for i in range(size)])


def in_place(blocks, mine):
    return jnp.stack([lax.select_n(mine, *[blocks[j ^ m] for m in range(4)]) for j in range(4)])


def exchange(pieces, axis, size, unit):
    mine = (lax.axis_index(axis) // unit) % 4
    kept, *sent = [lax.dynamic_index_in_dim(pieces, mine ^ d, 0, keepdims=False) for d in range(4)]
    return [kept] + [swapped(p, axis, size, (d + 1) * unit) for d, p in enumerate(sent)], mine


def collected(block, axis, size, unit):
    mine = (lax.axis_index(axis) // unit) % 4
    received = [swapped(block, axis, size, d * unit) for d in (1, 2, 3)]
    return in_place([block] + received, mine), received


def table_kernel(ordered, slots, send, pot, cell_scale, node_count, out, hot_high, hot_low):
    shape = (32, 128)
    row = lax.broadcasted_iota(jnp.int32, shape, 0)
    lane = lax.broadcasted_iota(jnp.int32, shape, 1)
    order = row * 128 + lane
    valid = order < ENTRIES
    entry = ordered[...] & 4095
    node = ordered[...] >> 12

    def along_rows(x, combine):
        for d in (1, 2, 4, 8, 16, 32, 64):
            x = jnp.where(lane >= d, combine(x, pltpu.roll(x, d, 1)), x)
        ends = jnp.broadcast_to(x[:, 127:128], shape)
        before = jnp.where(row >= 1, pltpu.roll(ends, 1, 0), 0.0)
        for d in (1, 2, 4, 8, 16):
            before = jnp.where(row >= d, combine(before, pltpu.roll(before, d, 0)), before)
        return combine(x, before)

    key = node.astype(jnp.float32)
    shifted = pltpu.roll(key, 1, 1)
    previous = jnp.where(lane == 0, pltpu.roll(shifted, 1, 0), shifted)
    head = (previous != key) | (order == 0)
    at = order.astype(jnp.float32)
    first = along_rows(jnp.where(head, at, 0.0), jnp.maximum)
    place = jnp.where(valid, at - first, 0.0)

    cell = (entry * CELL_MULTIPLIER) >> CELL_SHIFT
    position = entry + jnp.where(entry < CELLS * NPC, cell, CELLS) * (NPC_PAD - NPC)
    position = jnp.where(valid, position, 0).astype(jnp.float32)

    high_row = lax.broadcasted_iota(jnp.int32, (32, 128), 0)
    low_row = lax.broadcasted_iota(jnp.int32, (128, 128), 0)
    for q in range(ENTRY_CHUNKS):
        some = node[q : q + 1, :]
        hot_high[:, chunk(q)] = jnp.where(high_row == (some >> 7), 1.0, 0.0).astype(jnp.bfloat16)
        hot_low[:, chunk(q)] = jnp.where(low_row == (some & 127), 1.0, 0.0).astype(jnp.bfloat16)
    count = lax.dot_general(
        hot_high[...], hot_low[...], (((1,), (1,)), ((), ())), preferred_element_type=jnp.float32
    )
    up_to = along_rows(count, jnp.add)
    end = jnp.where(count > 0.0, up_to - 1.0, -1.0)

    nodes = slots[...]
    nodes = jnp.where(nodes >= NODES, nodes - NODES, nodes + GHOSTS)
    out[IDX_AT:POS_AT, :] = nodes.astype(jnp.float32)
    out[POS_AT:PLACE_AT, :] = position[:ENTRY_CHUNKS]
    out[PLACE_AT:END_AT, :] = place[:ENTRY_CHUNKS]
    out[END_AT:SEND_AT, :] = end[: EXT // 128]
    out[SEND_AT:POT_AT, :] = send[...].astype(jnp.float32)
    out[POT_AT:MISC_AT, :] = pot[...]
    ghost_entries = jnp.broadcast_to(up_to[GHOSTS // 128 - 1 : GHOSTS // 128, 127:128], (1, 128))
    longest = jnp.max(place) + 1.0
    one_lane = lane[:1]
    misc = jnp.where(one_lane == CELLS, node_count[0].astype(jnp.float32), 0.0)
    misc = jnp.where(one_lane == CELLS + 1, ghost_entries, misc)
    misc = jnp.where(one_lane == CELLS + 2, longest, misc)
    out[MISC_AT : MISC_AT + 1, :] = misc
    out[MISC_AT : MISC_AT + 1, 0:CELLS] = cell_scale[...]
    out[MISC_AT + 1 :, :] = jnp.zeros((START_AT - MISC_AT - 1, 128), jnp.float32)


def partition_table(cell_nodes, send_list, potential, cell_scale, node_count):
    shifted = jnp.where(cell_nodes >= NODES, cell_nodes - NODES, cell_nodes + GHOSTS)
    keys = jnp.concatenate([shifted.reshape(-1), send_list.reshape(-1) + GHOSTS])
    ordered = lax.sort(keys * 4096 + lax.iota(jnp.int32, ENTRIES))
    ordered = jnp.pad(ordered, (0, 4096 - ENTRIES), constant_values=PAD_NODE * 4096).reshape(32, 128)
    slots = jnp.pad(cell_nodes, ((0, 0), (0, NPC_PAD - NPC))).reshape(CELLS * CELL_CHUNKS, 128)
    vmem = pl.BlockSpec(memory_space=pltpu.VMEM)
    return pl.pallas_call(
        table_kernel,
        out_shape=jax.ShapeDtypeStruct((START_AT, 128), jnp.float32),
        in_specs=[vmem] * 5 + [pl.BlockSpec(memory_space=pltpu.SMEM)],
        out_specs=vmem,
        scratch_shapes=[
            pltpu.VMEM((32, ENTRY_PAD), jnp.bfloat16),
            pltpu.VMEM((128, ENTRY_PAD), jnp.bfloat16),
        ],
        compiler_params=pltpu.CompilerParams(vmem_limit_bytes=16 * 1024 * 1024),
    )(ordered, slots, send_list, potential.reshape(NODES // 128, 128), cell_scale.reshape(1, CELLS), node_count)


def gathered_tables(own_table, vectors):
    def next_step(both, members, receivers):
        tables, values = both[..., :START_AT, :], both[..., START_AT:, :]
        values = jnp.split(values, receivers, axis=-2)
        operand = jnp.stack([jnp.concatenate([tables, v], axis=-2) for v in values])
        return lax.all_to_all(operand, "mesh", 0, 0, axis_index_groups=groups_of(PARTS, members))

    values = vectors.reshape(PARTS * (NODES // 128), 128)
    both = next_step(jnp.concatenate([own_table, values]), (8, 16), 4)
    both = next_step(both, (2, 4), 4)
    both = next_step(both, (1,), 2)
    return both.transpose(2, 1, 0, 3, 4).reshape(PARTS, TABLE_CHUNKS * 128)


def chunk(c):
    return pl.ds(c * 128, 128)


def rows(g):
    return pl.ds(pl.multiple_of(g * 8, 8), 8)


def picked(sources, index):
    low = index & 127
    high = index >> 7
    total = jnp.zeros((8, 128), jnp.float32)
    for j, source in sources:
        total = jnp.where(high == j, jnp.take_along_axis(source, low, axis=1), total)
    return total


def filter_kernel(
    step_count, last, coef, table, field, matrix, out,
    mat_hi, mat_lo, idx, pos, place, end, send, scale, cur, prev, ext, vals, prod, arrived, w, halo, sums,
):
    lane = lax.broadcasted_iota(jnp.int32, (8, 128), 1)
    last_lane = jnp.full((8, 128), 127, jnp.int32)

    for k in range(CELL_CHUNKS):
        whole = matrix[k * 128 : (k + 1) * 128, :]
        high_part = whole.astype(jnp.bfloat16)
        low_part = (whole - high_part.astype(jnp.float32)).astype(jnp.bfloat16)
        mat_hi[k * 128 : (k + 1) * 128, :] = high_part
        mat_lo[k * 128 : (k + 1) * 128, :] = low_part

    def to_int(dest, first, count):
        for c in range(count):
            dest[:, chunk(c)] = table[:, chunk(first + c)].astype(jnp.int32)

    to_int(idx, IDX_AT, CELLS * CELL_CHUNKS)
    to_int(pos, POS_AT, ENTRY_CHUNKS)
    to_int(place, PLACE_AT, ENTRY_CHUNKS)
    to_int(end, END_AT, EXT // 128)
    to_int(send, SEND_AT, GHOSTS // 128)
    for c in range(CELLS):
        column = table[:, MISC_AT * 128 + c : MISC_AT * 128 + c + 1]
        scale[c * 32 : (c + 1) * 32, :] = jnp.broadcast_to(column, (PARTS, 128))

    def misc(c):
        return table[:, MISC_AT * 128 + CELLS + c : MISC_AT * 128 + CELLS + c + 1]

    short = jnp.max(misc(1)).astype(jnp.int32) <= FEW * 128
    short &= jnp.min(misc(1)).astype(jnp.int32) >= SKIP * 128
    short &= jnp.max(misc(2)).astype(jnp.int32) <= SHORT_RUN
    outside = jnp.zeros((PARTS, 128), jnp.float32)
    for n, (first, stop) in enumerate(WINDOWS):
        ends = table[:, chunk(END_AT + GHOSTS // 128 + n)]
        missed = (ends >= 0.0) & ((ends < first * 128.0) | (ends >= stop * 128.0))
        outside = jnp.maximum(outside, jnp.where(missed, 1.0, 0.0))
    short &= jnp.max(outside).astype(jnp.int32) == 0

    quarter = NODES // 4
    if last:
        for q in range(4):
            cur[:, q * quarter : (q + 1) * quarter] = field[q * 32 : (q + 1) * 32, :]
    else:
        live = misc(0).astype(jnp.int32)
        node = lax.broadcasted_iota(jnp.int32, (PARTS, NODES), 1)
        start = table[:, START_AT * 128 : TABLE_CHUNKS * 128]
        cur[...] = jnp.where(node < live, start, 0.0)
        prev[...] = jnp.zeros((PARTS, NODES), jnp.float32)

    def over_groups(body):
        def at(g, _):
            body(g, rows(g))
            return 0

        lax.fori_loop(0, GROUPS, at, 0)

    def wrap(values, k):
        c = chunk(k)
        halo[2:34, c] = values
        halo[0:2, c] = values[30:32]
        halo[34:36, c] = values[0:2]

    def products_of(g):
        return [
            (c * CELL_CHUNKS + k, prod[pl.ds(pl.multiple_of(c * 32 + g * 8, 8), 8), chunk(k)])
            for c in range(CELLS)
            for k in range(CELL_CHUNKS)
        ]

    def into_order(r, sources, first, stop):
        for q in range(first, stop):
            w[r, chunk(q)] = picked(sources, pos[r, chunk(q)])

    def partial_runs(places, longest):
        xs = [w[r, chunk(q)] for r, q in places]
        near = [jnp.minimum(place[r, chunk(q)], lane) for r, q in places]
        for d in [1 << k for k in range(7) if (1 << k) < longest]:
            back = (lane - d) & 127
            moved = [jnp.take_along_axis(x, back, axis=1) for x in xs]
            xs = [x + jnp.where(a >= d, m, 0.0) for x, a, m in zip(xs, near, moved)]
        for (r, q), x in zip(places, xs):
            w[r, chunk(q)] = x

    def joined_runs(r, first, stop):
        xs = [w[r, chunk(q)] for q in range(first, stop)]
        done = [(first, xs[0])]
        for q, x, before in zip(range(first + 1, stop), xs[1:], xs):
            carry = jnp.take_along_axis(before, last_lane, axis=1)
            done.append((q, x + jnp.where(place[r, chunk(q)] > lane, carry, 0.0)))
        return done

    def chained_runs(r):
        carry = jnp.zeros((8, 128), jnp.float32)
        done = []
        for q in range(ENTRY_CHUNKS):
            x = w[r, chunk(q)]
            total = jnp.take_along_axis(x, last_lane, axis=1)
            goes_on = place[r, chunk(q)] > lane
            through = jnp.take_along_axis(jnp.where(goes_on, 1.0, 0.0), last_lane, axis=1)
            done.append((q, x + jnp.where(goes_on, carry, 0.0)))
            carry = total + through * carry
        return done

    def run_ends(r, sources, node_first, windows):
        for n, (first, stop) in enumerate(windows):
            inside = [(q, source) for q, source in sources if first <= q < stop]
            sums[r, chunk(n)] = picked(inside, end[r, chunk(node_first + n)])

    anywhere = ((0, ENTRY_CHUNKS),)

    def with_arrivals(g, r):
        base = CELLS * CELL_CHUNKS
        return products_of(g) + [(base + k, arrived[r, chunk(k)]) for k in range(4)]

    fixed = [pl.ds(g * 8, 8) for g in range(GROUPS)]

    def in_order_and_summed(sources_of):
        def at(g, r):
            into_order(r, sources_of(g, r), 0, ENTRY_CHUNKS)
            partial_runs([(r, q) for q in range(ENTRY_CHUNKS)], 128)

        over_groups(at)

    def ghost_sums():
        for g, r in enumerate(fixed):
            into_order(r, products_of(g), 0, FEW)
        partial_runs([(r, q) for r in fixed for q in range(FEW)], SHORT_RUN)
        for r in fixed:
            run_ends(r, joined_runs(r, 0, FEW), 0, ((0, FEW),) * 4)

    def ghost_sums_any():
        in_order_and_summed(lambda g, r: products_of(g))
        over_groups(lambda g, r: run_ends(r, chained_runs(r), 0, anywhere * 4))

    def own_sums():
        over_groups(lambda g, r: into_order(r, with_arrivals(g, r), SKIP, ENTRY_CHUNKS))
        for r in fixed:
            partial_runs([(r, q) for q in range(SKIP, ENTRY_CHUNKS)], SHORT_RUN)
        over_groups(lambda g, r: run_ends(r, joined_runs(r, SKIP, ENTRY_CHUNKS), 4, WINDOWS))

    def own_sums_any():
        in_order_and_summed(with_arrivals)
        over_groups(lambda g, r: run_ends(r, chained_runs(r), 4, anywhere * 16))

    def apply():
        def outgoing(g, r):
            sources = [(j, cur[r, chunk(j)]) for j in range(NODES // 128)]
            for k in range(4):
                sums[r, chunk(k)] = picked(sources, send[r, chunk(k)])

        for g in range(GROUPS):
            outgoing(g, pl.ds(g * 8, 8))
        for k in range(4):
            wrap(sums[:, k * 128 : (k + 1) * 128], k)
        for k, o in enumerate(OFFSETS):
            ext[:, k * 128 : (k + 1) * 128] = halo[2 + o : 34 + o, k * 128 : (k + 1) * 128]
        ext[:, GHOSTS:] = cur[...]

        def gather(g, r):
            sources = [(j, ext[r, chunk(j)]) for j in range(EXT // 128)]

            for c in range(CELLS):
                there = pl.ds(pl.multiple_of(c * 32 + g * 8, 8), 8)
                for k in range(CELL_CHUNKS):
                    vals[there, chunk(k)] = picked(sources, idx[r, chunk(c * CELL_CHUNKS + k)])

        over_groups(gather)

        x = vals[...]
        high = x.astype(jnp.bfloat16)
        low = (x - high.astype(jnp.float32)).astype(jnp.bfloat16)

        def dot(a, b):
            return jnp.dot(a, b, preferred_element_type=jnp.float32)

        y = dot(high, mat_hi[...]) + (dot(low, mat_hi[...]) + dot(high, mat_lo[...]))
        for k in range(CELL_CHUNKS):
            prod[:, k * 128 : (k + 1) * 128] = y[:, k * 128 : (k + 1) * 128] * scale[...]

        pl.when(short)(ghost_sums)
        pl.when(~short)(ghost_sums_any)
        for k in range(4):
            wrap(sums[:, k * 128 : (k + 1) * 128], k)
        for k, o in enumerate(OFFSETS):
            arrived[:, k * 128 : (k + 1) * 128] = halo[2 - o : 34 - o, k * 128 : (k + 1) * 128]

        pl.when(short)(own_sums)
        pl.when(~short)(own_sums_any)

    def step(i, _):
        apply()
        degree = lax.rem(i, DEGREE)
        gain = coef[degree]
        back = coef[DEGREE + degree]
        centre = coef[2 * DEGREE]
        for c in range(NODES // 128):
            here = chunk(c)
            v = cur[:, here]
            hv = sums[:, here] + table[:, chunk(POT_AT + c)] * v
            following = gain * (hv - centre * v)
            following = jnp.where(degree == 0, following, following - back * prev[:, here])
            prev[:, here] = v
            cur[:, here] = following
        return 0

    if last:
        apply()
        for c in range(NODES // 128):
            cur[:, chunk(c)] = sums[:, chunk(c)] + table[:, chunk(POT_AT + c)] * cur[:, chunk(c)]
    else:
        lax.fori_loop(0, step_count, step, 0)
    for q in range(4):
        out[q * 32 : (q + 1) * 32, :] = cur[:, q * quarter : (q + 1) * quarter]


def run_filter(coef, table, field, cell_matrix, step_count, last):
    padded = jnp.pad(cell_matrix, ((0, NPC_PAD - NPC), (0, NPC_PAD - NPC)))
    vmem = pl.BlockSpec(memory_space=pltpu.VMEM)
    f32, i32 = jnp.float32, jnp.int32
    cells = CELLS * PARTS
    return pl.pallas_call(
        functools.partial(filter_kernel, step_count, last),
        out_shape=jax.ShapeDtypeStruct((4 * PARTS, NODES // 4), f32),
        in_specs=[pl.BlockSpec(memory_space=pltpu.SMEM)] + [vmem] * 3,
        out_specs=vmem,
        scratch_shapes=[
            pltpu.VMEM((NPC_PAD, NPC_PAD), jnp.bfloat16),
            pltpu.VMEM((NPC_PAD, NPC_PAD), jnp.bfloat16),
            pltpu.VMEM((PARTS, CELLS * NPC_PAD), i32),
            pltpu.VMEM((PARTS, ENTRY_PAD), i32),
            pltpu.VMEM((PARTS, ENTRY_PAD), i32),
            pltpu.VMEM((PARTS, EXT), i32),
            pltpu.VMEM((PARTS, GHOSTS), i32),
            pltpu.VMEM((cells, 128), f32),
            pltpu.VMEM((PARTS, NODES), f32),
            pltpu.VMEM((PARTS, NODES), f32),
            pltpu.VMEM((PARTS, EXT), f32),
            pltpu.VMEM((cells, NPC_PAD), f32),
            pltpu.VMEM((cells, NPC_PAD), f32),
            pltpu.VMEM((PARTS, GHOSTS), f32),
            pltpu.VMEM((PARTS, ENTRY_PAD), f32),
            pltpu.VMEM((40, GHOSTS), f32),
            pltpu.VMEM((PARTS, NODES), f32),
        ],
        compiler_params=pltpu.CompilerParams(vmem_limit_bytes=48 * 1024 * 1024),
        cost_estimate=pl.CostEstimate(
            flops=step_count * 15_000_000_000, bytes_accessed=step_count * 50_000_000, transcendentals=0
        ),
    )(coef, table, field, padded)


def coefficients(filter_bounds):
    lowest, wanted_top, upper = filter_bounds[0], filter_bounds[1], filter_bounds[2]
    half_width = (upper - wanted_top) / 2.0
    centre = (upper + wanted_top) / 2.0
    sigma = half_width / (lowest - centre)
    ratio = 2.0 / sigma
    gains, backs = [sigma / half_width], [jnp.zeros_like(sigma)]
    for _ in range(DEGREE - 1):
        following = 1.0 / (ratio - sigma)
        gains.append(2.0 * following / half_width)
        backs.append(sigma * following)
        sigma = following
    return jnp.stack(gains + backs + [centre, centre])


def body(vectors, potential, cell_scale, cell_matrix, cell_nodes, send_list, node_count, filter_bounds):
    own_table = partition_table(cell_nodes, send_list[0], potential, cell_scale, node_count)
    table = gathered_tables(own_table, vectors)

    coef = coefficients(filter_bounds)
    quarters = groups_of(16 * PARTS, (1, 2, 4, 8, 16, PARTS, 2 * PARTS))

    def to_quarters(field):
        pieces = field.reshape(4 * PARTS, NODES // 512, 128)
        pieces = lax.all_to_all(pieces, ("band", "mesh"), 0, 0, axis_index_groups=quarters)
        return pieces.reshape(4 * PARTS, NODES // 4)

    f = run_filter(coef, table, jnp.zeros((8, 128), jnp.float32), cell_matrix, 2 * DEGREE, False)
    f_quarter = to_quarters(f)
    g = run_filter(coef, table, f, cell_matrix, 1, True)
    left = to_quarters(g)
    band_rows = vectors.shape[0]
    right, received = collected(f_quarter, "band", 16, 4)
    right = right.reshape(16 * band_rows, NODES // 4)
    partial = lax.dot_general(left, right, (((1,), (1,)), ((), ())), precision=HIGHEST)

    plane = groups_of(PARTS, (1, 2, 4))
    partial = partial.reshape(4, 8, band_rows // 8, 16 * band_rows).transpose(1, 0, 2, 3)
    partial = lax.all_to_all(partial, "mesh", 0, 0, axis_index_groups=plane).sum(0)
    along_z = groups_of(16 * PARTS, (8, 16, PARTS, 2 * PARTS))
    partial = jnp.broadcast_to(partial[:, None], (4, 4) + partial.shape[1:])
    partial = partial.reshape((16,) + partial.shape[2:])
    block = lax.all_to_all(partial, ("band", "mesh"), 0, 0, axis_index_groups=along_z).sum(0)
    block = block / (NODES * PARTS)
    hproj = spread(block, "mesh", PARTS, (1, 2, 4))
    f_quarter, _ = lax.optimization_barrier((f_quarter, received[0]))
    quarter_rows, mine = exchange(f_quarter.reshape(4, band_rows, NODES // 4), "band", 16, 1)
    quarter_rows, hproj = lax.optimization_barrier((quarter_rows, hproj))
    filtered = in_place(quarter_rows, mine).transpose(1, 0, 2).reshape(band_rows, NODES)
    hproj = hproj.reshape(band_rows, 16 * band_rows)
    return filtered, hproj


def solution(mesh):
    placed = (
        P("band", "mesh"),
        P("mesh"),
        P("mesh"),
        P(),
        P("mesh", None),
        P("mesh", None, None),
        P("mesh"),
        P(),
    )
    return jax.shard_map(
        body,
        mesh=mesh,
        in_specs=placed,
        out_specs=(P("band", "mesh"), P("band", None)),
        check_vma=False,
    )
```

```python
import functools

import jax
import jax.numpy as jnp
from jax import lax
from jax.experimental import pallas as pl
from jax.experimental.pallas import tpu as pltpu
from jax.sharding import PartitionSpec as P

DEGREE = 3
OFFSETS = (-2, -1, 1, 2)
HIGHEST = lax.Precision.HIGHEST

PARTS = 32
GROUPS = PARTS // 8
NODES = 2048
SLOTS = 128
GHOSTS = 4 * SLOTS
EXT = GHOSTS + NODES
CELLS = 8
NPC = 343
NPC_PAD = 384
CELL_CHUNKS = NPC_PAD // 128
ENTRIES = CELLS * NPC + GHOSTS
ENTRY_CHUNKS = 26
ENTRY_PAD = ENTRY_CHUNKS * 128
PAD_NODE = 4095
CELL_MULTIPLIER, CELL_SHIFT = 6115, 21
FEW = 5
SKIP = 3
SHORT_RUN = 16
WINDOWS = (
    (3, 8), (4, 11), (6, 13), (7, 16), (8, 19), (10, 21), (11, 24), (12, 26),
    (13, 26), (15, 26), (16, 26), (18, 26), (19, 26), (20, 26), (22, 26), (23, 26),
)

IDX_AT = 0
POS_AT = IDX_AT + CELLS * CELL_CHUNKS
PLACE_AT = POS_AT + ENTRY_CHUNKS
END_AT = PLACE_AT + ENTRY_CHUNKS
SEND_AT = END_AT + EXT // 128
POT_AT = SEND_AT + GHOSTS // 128
MISC_AT = POT_AT + NODES // 128
START_AT = MISC_AT + 4
TABLE_CHUNKS = START_AT + NODES // 128


def groups_of(size, bits):
    mask = sum(bits)
    members = {}
    for i in range(size):
        members.setdefault(i & ~mask, []).append(i)
    return list(members.values())


def spread(block, axis, size, bits):
    members = groups_of(size, bits)
    copies = jnp.broadcast_to(block[None], (len(members[0]),) + block.shape)
    return lax.all_to_all(copies, axis, 0, 0, axis_index_groups=members)


def swapped(block, axis, size, distance):
    return lax.ppermute(block, axis, [(i ^ distance, i) for i in range(size)])


def in_place(blocks, mine):
    return jnp.stack([lax.select_n(mine, *[blocks[j ^ m] for m in range(4)]) for j in range(4)])


def exchange(pieces, axis, size, unit):
    mine = (lax.axis_index(axis) // unit) % 4
    kept, *sent = [lax.dynamic_index_in_dim(pieces, mine ^ d, 0, keepdims=False) for d in range(4)]
    return [kept] + [swapped(p, axis, size, (d + 1) * unit) for d, p in enumerate(sent)], mine


def table_kernel(
    ordered, slots_in, send_in, pot_in, cell_scale_in, node_count, out,
    hot_high, hot_low, slots, send, pot, cell_scale, arrival,
):
    fetched = ((slots_in, slots), (send_in, send), (pot_in, pot), (cell_scale_in, cell_scale))
    fetches = [pltpu.make_async_copy(a, b, arrival.at[i]) for i, (a, b) in enumerate(fetched)]
    for fetch in fetches:
        fetch.start()
    shape = (32, 128)
    row = lax.broadcasted_iota(jnp.int32, shape, 0)
    lane = lax.broadcasted_iota(jnp.int32, shape, 1)
    order = row * 128 + lane
    valid = order < ENTRIES
    entry = ordered[...] & 4095
    node = ordered[...] >> 12

    def along_rows(x, combine):
        for d in (1, 2, 4, 8, 16, 32, 64):
            x = jnp.where(lane >= d, combine(x, pltpu.roll(x, d, 1)), x)
        ends = jnp.broadcast_to(x[:, 127:128], shape)
        before = jnp.where(row >= 1, pltpu.roll(ends, 1, 0), 0.0)
        for d in (1, 2, 4, 8, 16):
            before = jnp.where(row >= d, combine(before, pltpu.roll(before, d, 0)), before)
        return combine(x, before)

    key = node.astype(jnp.float32)
    shifted = pltpu.roll(key, 1, 1)
    previous = jnp.where(lane == 0, pltpu.roll(shifted, 1, 0), shifted)
    head = (previous != key) | (order == 0)
    at = order.astype(jnp.float32)
    first = along_rows(jnp.where(head, at, 0.0), jnp.maximum)
    place = jnp.where(valid, at - first, 0.0)

    cell = (entry * CELL_MULTIPLIER) >> CELL_SHIFT
    position = entry + jnp.where(entry < CELLS * NPC, cell, CELLS) * (NPC_PAD - NPC)
    position = jnp.where(valid, position, 0).astype(jnp.float32)

    high_row = lax.broadcasted_iota(jnp.int32, (32, 128), 0)
    low_row = lax.broadcasted_iota(jnp.int32, (128, 128), 0)
    for q in range(ENTRY_CHUNKS):
        some = node[q : q + 1, :]
        hot_high[:, chunk(q)] = jnp.where(high_row == (some >> 7), 1.0, 0.0).astype(jnp.bfloat16)
        hot_low[:, chunk(q)] = jnp.where(low_row == (some & 127), 1.0, 0.0).astype(jnp.bfloat16)
    count = lax.dot_general(
        hot_high[...], hot_low[...], (((1,), (1,)), ((), ())), preferred_element_type=jnp.float32
    )
    up_to = along_rows(count, jnp.add)
    end = jnp.where(count > 0.0, up_to - 1.0, -1.0)

    for fetch in fetches:
        fetch.wait()
    nodes = slots[...]
    nodes = jnp.where(nodes >= NODES, nodes - NODES, nodes + GHOSTS).astype(jnp.float32)
    out[IDX_AT:POS_AT, :] = jnp.zeros((POS_AT - IDX_AT, 128), jnp.float32)
    for c in range(CELLS):
        for k in range(CELL_CHUNKS):
            at, width = IDX_AT + c * CELL_CHUNKS + k, min(128, NPC - k * 128)
            out[at : at + 1, 0:width] = nodes[c : c + 1, k * 128 : k * 128 + width]
    out[POS_AT:PLACE_AT, :] = position[:ENTRY_CHUNKS]
    out[PLACE_AT:END_AT, :] = place[:ENTRY_CHUNKS]
    out[END_AT:SEND_AT, :] = end[: EXT // 128]
    out[SEND_AT:POT_AT, :] = send[...].astype(jnp.float32)
    out[POT_AT:MISC_AT, :] = pot[...]
    ghost_entries = jnp.broadcast_to(up_to[GHOSTS // 128 - 1 : GHOSTS // 128, 127:128], (1, 128))
    longest = jnp.max(place) + 1.0
    one_lane = lane[:1]
    misc = jnp.where(one_lane == CELLS, node_count[0].astype(jnp.float32), 0.0)
    misc = jnp.where(one_lane == CELLS + 1, ghost_entries, misc)
    misc = jnp.where(one_lane == CELLS + 2, longest, misc)
    out[MISC_AT : MISC_AT + 1, :] = misc
    out[MISC_AT : MISC_AT + 1, 0:CELLS] = cell_scale[...]
    out[MISC_AT + 1 :, :] = jnp.zeros((START_AT - MISC_AT - 1, 128), jnp.float32)


def partition_table(cell_nodes, send_list, potential, cell_scale, node_count):
    shifted = jnp.where(cell_nodes >= NODES, cell_nodes - NODES, cell_nodes + GHOSTS)
    keys = jnp.concatenate([shifted.reshape(-1), send_list.reshape(-1) + GHOSTS])
    ordered = lax.sort(keys * 4096 + lax.iota(jnp.int32, ENTRIES))
    ordered = jnp.pad(ordered, (0, 4096 - ENTRIES), constant_values=PAD_NODE * 4096).reshape(32, 128)
    vmem = pl.BlockSpec(memory_space=pltpu.VMEM)
    return pl.pallas_call(
        table_kernel,
        out_shape=jax.ShapeDtypeStruct((START_AT, 128), jnp.float32),
        in_specs=[vmem] + [pl.BlockSpec(memory_space=pltpu.HBM)] * 4 + [pl.BlockSpec(memory_space=pltpu.SMEM)],
        out_specs=vmem,
        scratch_shapes=[
            pltpu.VMEM((32, ENTRY_PAD), jnp.bfloat16),
            pltpu.VMEM((128, ENTRY_PAD), jnp.bfloat16),
            pltpu.VMEM((CELLS, NPC), jnp.int32),
            pltpu.VMEM((4, SLOTS), jnp.int32),
            pltpu.VMEM((NODES // 128, 128), jnp.float32),
            pltpu.VMEM((1, CELLS), jnp.float32),
            pltpu.SemaphoreType.DMA((4,)),
        ],
        compiler_params=pltpu.CompilerParams(vmem_limit_bytes=16 * 1024 * 1024),
    )(ordered, cell_nodes, send_list, potential.reshape(NODES // 128, 128), cell_scale.reshape(1, CELLS), node_count)


def gathered_tables(own_table, vectors):
    def next_step(both, members, receivers):
        tables, values = both[..., :START_AT, :], both[..., START_AT:, :]
        values = jnp.split(values, receivers, axis=-2)
        operand = jnp.stack([jnp.concatenate([tables, v], axis=-2) for v in values])
        return lax.all_to_all(operand, "mesh", 0, 0, axis_index_groups=groups_of(PARTS, members))

    values = vectors.reshape(PARTS * (NODES // 128), 128)
    both = next_step(jnp.concatenate([own_table, values]), (8, 16), 4)
    both = next_step(both, (2, 4), 4)
    both = next_step(both, (1,), 2)
    return both.transpose(2, 1, 0, 3, 4).reshape(PARTS, TABLE_CHUNKS * 128)


def chunk(c):
    return pl.ds(c * 128, 128)


def rows(g):
    return pl.ds(pl.multiple_of(g * 8, 8), 8)


def picked(sources, index):
    low = index & 127
    high = index >> 7
    total = jnp.zeros((8, 128), jnp.float32)
    for j, source in sources:
        total = jnp.where(high == j, jnp.take_along_axis(source, low, axis=1), total)
    return total


def filter_kernel(
    step_count, last, coef, table, field, matrix, out,
    mat_hi, mat_lo, idx, pos, place, end, send, scale, cur, prev, ext, vals, prod, arrived, w, halo, sums,
):
    lane = lax.broadcasted_iota(jnp.int32, (8, 128), 1)
    last_lane = jnp.full((8, 128), 127, jnp.int32)

    for k in range(CELL_CHUNKS):
        whole = matrix[k * 128 : (k + 1) * 128, :]
        high_part = whole.astype(jnp.bfloat16)
        low_part = (whole - high_part.astype(jnp.float32)).astype(jnp.bfloat16)
        mat_hi[k * 128 : (k + 1) * 128, :] = high_part
        mat_lo[k * 128 : (k + 1) * 128, :] = low_part

    def to_int(dest, first, count):
        for c in range(count):
            dest[:, chunk(c)] = table[:, chunk(first + c)].astype(jnp.int32)

    to_int(idx, IDX_AT, CELLS * CELL_CHUNKS)
    to_int(pos, POS_AT, ENTRY_CHUNKS)
    to_int(place, PLACE_AT, ENTRY_CHUNKS)
    to_int(end, END_AT, EXT // 128)
    to_int(send, SEND_AT, GHOSTS // 128)
    for c in range(CELLS):
        column = table[:, MISC_AT * 128 + c : MISC_AT * 128 + c + 1]
        scale[c * 32 : (c + 1) * 32, :] = jnp.broadcast_to(column, (PARTS, 128))

    def misc(c):
        return table[:, MISC_AT * 128 + CELLS + c : MISC_AT * 128 + CELLS + c + 1]

    short = jnp.max(misc(1)).astype(jnp.int32) <= FEW * 128
    short &= jnp.min(misc(1)).astype(jnp.int32) >= SKIP * 128
    short &= jnp.max(misc(2)).astype(jnp.int32) <= SHORT_RUN
    outside = jnp.zeros((PARTS, 128), jnp.float32)
    for n, (first, stop) in enumerate(WINDOWS):
        ends = table[:, chunk(END_AT + GHOSTS // 128 + n)]
        missed = (ends >= 0.0) & ((ends < first * 128.0) | (ends >= stop * 128.0))
        outside = jnp.maximum(outside, jnp.where(missed, 1.0, 0.0))
    short &= jnp.max(outside).astype(jnp.int32) == 0

    quarter = NODES // 4
    if last:
        for q in range(4):
            cur[:, q * quarter : (q + 1) * quarter] = field[q * 32 : (q + 1) * 32, :]
    else:
        live = misc(0).astype(jnp.int32)
        node = lax.broadcasted_iota(jnp.int32, (PARTS, NODES), 1)
        start = table[:, START_AT * 128 : TABLE_CHUNKS * 128]
        cur[...] = jnp.where(node < live, start, 0.0)
        prev[...] = jnp.zeros((PARTS, NODES), jnp.float32)

    def over_groups(body, unroll=1):
        def at(g, _):
            body(g, rows(g))
            return 0

        lax.fori_loop(0, GROUPS, at, 0, unroll=unroll)

    def wrap(values, k):
        c = chunk(k)
        halo[2:34, c] = values
        halo[0:2, c] = values[30:32]
        halo[34:36, c] = values[0:2]

    def products_of(g):
        return [
            (c * CELL_CHUNKS + k, prod[pl.ds(pl.multiple_of(c * 32 + g * 8, 8), 8), chunk(k)])
            for c in range(CELLS)
            for k in range(CELL_CHUNKS)
        ]

    def into_order(r, sources, first, stop):
        for q in range(first, stop):
            w[r, chunk(q)] = picked(sources, pos[r, chunk(q)])

    def partial_runs(places, longest):
        xs = [w[r, chunk(q)] for r, q in places]
        near = [jnp.minimum(place[r, chunk(q)], lane) for r, q in places]
        for d in [1 << k for k in range(7) if (1 << k) < longest]:
            back = (lane - d) & 127
            moved = [jnp.take_along_axis(x, back, axis=1) for x in xs]
            xs = [x + jnp.where(a >= d, m, 0.0) for x, a, m in zip(xs, near, moved)]
        for (r, q), x in zip(places, xs):
            w[r, chunk(q)] = x

    def joined_runs(r, first, stop):
        xs = [w[r, chunk(q)] for q in range(first, stop)]
        done = [(first, xs[0])]
        for q, x, before in zip(range(first + 1, stop), xs[1:], xs):
            carry = jnp.take_along_axis(before, last_lane, axis=1)
            done.append((q, x + jnp.where(place[r, chunk(q)] > lane, carry, 0.0)))
        return done

    def chained_runs(r):
        carry = jnp.zeros((8, 128), jnp.float32)
        done = []
        for q in range(ENTRY_CHUNKS):
            x = w[r, chunk(q)]
            total = jnp.take_along_axis(x, last_lane, axis=1)
            goes_on = place[r, chunk(q)] > lane
            through = jnp.take_along_axis(jnp.where(goes_on, 1.0, 0.0), last_lane, axis=1)
            done.append((q, x + jnp.where(goes_on, carry, 0.0)))
            carry = total + through * carry
        return done

    def run_ends(r, sources, node_first, windows):
        for n, (first, stop) in enumerate(windows):
            inside = [(q, source) for q, source in sources if first <= q < stop]
            sums[r, chunk(n)] = picked(inside, end[r, chunk(node_first + n)])

    anywhere = ((0, ENTRY_CHUNKS),)

    def with_arrivals(g, r):
        base = CELLS * CELL_CHUNKS
        return products_of(g) + [(base + k, arrived[r, chunk(k)]) for k in range(4)]

    fixed = [pl.ds(g * 8, 8) for g in range(GROUPS)]

    def in_order_and_summed(sources_of):
        def at(g, r):
            into_order(r, sources_of(g, r), 0, ENTRY_CHUNKS)
            partial_runs([(r, q) for q in range(ENTRY_CHUNKS)], 128)

        over_groups(at)

    def ghost_sums():
        for g, r in enumerate(fixed):
            into_order(r, products_of(g), 0, FEW)
        partial_runs([(r, q) for r in fixed for q in range(FEW)], SHORT_RUN)
        for r in fixed:
            run_ends(r, joined_runs(r, 0, FEW), 0, ((0, FEW),) * 4)

    def ghost_sums_any():
        in_order_and_summed(lambda g, r: products_of(g))
        over_groups(lambda g, r: run_ends(r, chained_runs(r), 0, anywhere * 4))

    def own_sums():
        over_groups(lambda g, r: into_order(r, with_arrivals(g, r), SKIP, ENTRY_CHUNKS), 2)
        for r in fixed:
            partial_runs([(r, q) for q in range(SKIP, ENTRY_CHUNKS)], SHORT_RUN)
        over_groups(lambda g, r: run_ends(r, joined_runs(r, SKIP, ENTRY_CHUNKS), 4, WINDOWS), 2)

    def own_sums_any():
        in_order_and_summed(with_arrivals)
        over_groups(lambda g, r: run_ends(r, chained_runs(r), 4, anywhere * 16))

    def apply():
        def outgoing(g, r):
            sources = [(j, cur[r, chunk(j)]) for j in range(NODES // 128)]
            for k in range(4):
                sums[r, chunk(k)] = picked(sources, send[r, chunk(k)])

        for g in range(GROUPS):
            outgoing(g, pl.ds(g * 8, 8))
        for k in range(4):
            wrap(sums[:, k * 128 : (k + 1) * 128], k)
        for k, o in enumerate(OFFSETS):
            ext[:, k * 128 : (k + 1) * 128] = halo[2 + o : 34 + o, k * 128 : (k + 1) * 128]
        ext[:, GHOSTS:] = cur[...]

        def gather(g, r):
            sources = [(j, ext[r, chunk(j)]) for j in range(EXT // 128)]

            for c in range(CELLS):
                there = pl.ds(pl.multiple_of(c * 32 + g * 8, 8), 8)
                for k in range(CELL_CHUNKS):
                    vals[there, chunk(k)] = picked(sources, idx[r, chunk(c * CELL_CHUNKS + k)])

        over_groups(gather, 2)

        x = vals[...]
        high = x.astype(jnp.bfloat16)
        low = (x - high.astype(jnp.float32)).astype(jnp.bfloat16)

        def dot(a, b):
            return jnp.dot(a, b, preferred_element_type=jnp.float32)

        y = dot(high, mat_hi[...]) + (dot(low, mat_hi[...]) + dot(high, mat_lo[...]))
        for k in range(CELL_CHUNKS):
            prod[:, k * 128 : (k + 1) * 128] = y[:, k * 128 : (k + 1) * 128] * scale[...]

        pl.when(short)(ghost_sums)
        pl.when(~short)(ghost_sums_any)
        for k in range(4):
            wrap(sums[:, k * 128 : (k + 1) * 128], k)
        for k, o in enumerate(OFFSETS):
            arrived[:, k * 128 : (k + 1) * 128] = halo[2 - o : 34 - o, k * 128 : (k + 1) * 128]

        pl.when(short)(own_sums)
        pl.when(~short)(own_sums_any)

    def step(i, _):
        apply()
        degree = lax.rem(i, DEGREE)
        gain = coef[degree]
        back = coef[DEGREE + degree]
        centre = coef[2 * DEGREE]
        for c in range(NODES // 128):
            here = chunk(c)
            v = cur[:, here]
            hv = sums[:, here] + table[:, chunk(POT_AT + c)] * v
            following = gain * (hv - centre * v)
            following = jnp.where(degree == 0, following, following - back * prev[:, here])
            prev[:, here] = v
            cur[:, here] = following
        return 0

    if last:
        apply()
        for c in range(NODES // 128):
            cur[:, chunk(c)] = sums[:, chunk(c)] + table[:, chunk(POT_AT + c)] * cur[:, chunk(c)]
    else:
        lax.fori_loop(0, step_count, step, 0)
    for q in range(4):
        out[q * 32 : (q + 1) * 32, :] = cur[:, q * quarter : (q + 1) * quarter]


def run_filter(coef, table, field, cell_matrix, step_count, last):
    padded = jnp.pad(cell_matrix, ((0, NPC_PAD - NPC), (0, NPC_PAD - NPC)))
    vmem = pl.BlockSpec(memory_space=pltpu.VMEM)
    f32, i32 = jnp.float32, jnp.int32
    cells = CELLS * PARTS
    return pl.pallas_call(
        functools.partial(filter_kernel, step_count, last),
        out_shape=jax.ShapeDtypeStruct((4 * PARTS, NODES // 4), f32),
        in_specs=[pl.BlockSpec(memory_space=pltpu.SMEM)] + [vmem] * 3,
        out_specs=vmem,
        scratch_shapes=[
            pltpu.VMEM((NPC_PAD, NPC_PAD), jnp.bfloat16),
            pltpu.VMEM((NPC_PAD, NPC_PAD), jnp.bfloat16),
            pltpu.VMEM((PARTS, CELLS * NPC_PAD), i32),
            pltpu.VMEM((PARTS, ENTRY_PAD), i32),
            pltpu.VMEM((PARTS, ENTRY_PAD), i32),
            pltpu.VMEM((PARTS, EXT), i32),
            pltpu.VMEM((PARTS, GHOSTS), i32),
            pltpu.VMEM((cells, 128), f32),
            pltpu.VMEM((PARTS, NODES), f32),
            pltpu.VMEM((PARTS, NODES), f32),
            pltpu.VMEM((PARTS, EXT), f32),
            pltpu.VMEM((cells, NPC_PAD), f32),
            pltpu.VMEM((cells, NPC_PAD), f32),
            pltpu.VMEM((PARTS, GHOSTS), f32),
            pltpu.VMEM((PARTS, ENTRY_PAD), f32),
            pltpu.VMEM((40, GHOSTS), f32),
            pltpu.VMEM((PARTS, NODES), f32),
        ],
        compiler_params=pltpu.CompilerParams(vmem_limit_bytes=48 * 1024 * 1024),
        cost_estimate=pl.CostEstimate(
            flops=step_count * 15_000_000_000, bytes_accessed=step_count * 50_000_000, transcendentals=0
        ),
    )(coef, table, field, padded)


def coefficients(filter_bounds):
    lowest, wanted_top, upper = filter_bounds[0], filter_bounds[1], filter_bounds[2]
    half_width = (upper - wanted_top) / 2.0
    centre = (upper + wanted_top) / 2.0
    sigma = half_width / (lowest - centre)
    ratio = 2.0 / sigma
    gains, backs = [sigma / half_width], [jnp.zeros_like(sigma)]
    for _ in range(DEGREE - 1):
        following = 1.0 / (ratio - sigma)
        gains.append(2.0 * following / half_width)
        backs.append(sigma * following)
        sigma = following
    return jnp.stack(gains + backs + [centre, centre])


def body(vectors, potential, cell_scale, cell_matrix, cell_nodes, send_list, node_count, filter_bounds):
    own_table = partition_table(cell_nodes, send_list[0], potential, cell_scale, node_count)
    table = gathered_tables(own_table, vectors)

    coef = coefficients(filter_bounds)
    quarters = groups_of(16 * PARTS, (1, 2, 4, 8, 16, PARTS, 2 * PARTS))

    def to_quarters(field):
        pieces = field.reshape(4 * PARTS, NODES // 512, 128)
        pieces = lax.all_to_all(pieces, ("band", "mesh"), 0, 0, axis_index_groups=quarters)
        return pieces.reshape(4 * PARTS, NODES // 4)

    f = run_filter(coef, table, jnp.zeros((8, 128), jnp.float32), cell_matrix, 2 * DEGREE, False)
    f_quarter = to_quarters(f)
    g = run_filter(coef, table, f, cell_matrix, 1, True)
    left = to_quarters(g)
    band_rows = vectors.shape[0]
    received = [swapped(f_quarter, "band", 16, 4 * d) for d in (1, 2, 3)]
    products = [
        lax.dot_general(left, right, (((1,), (1,)), ((), ())), precision=HIGHEST)
        for right in (f_quarter, *received)
    ]
    partial = in_place(products, lax.axis_index("band") // 4)

    plane = groups_of(PARTS, (1, 2, 4))
    partial = partial.reshape(4, 4, 8, band_rows // 8, 4 * band_rows).transpose(2, 1, 3, 0, 4)
    partial = partial.reshape(8, 4, band_rows // 8, 16 * band_rows)
    partial = lax.all_to_all(partial, "mesh", 0, 0, axis_index_groups=plane).sum(0)
    along_z = groups_of(16 * PARTS, (8, 16, PARTS, 2 * PARTS))
    partial = jnp.broadcast_to(partial[:, None], (4, 4) + partial.shape[1:])
    partial = partial.reshape((16,) + partial.shape[2:])
    block = lax.all_to_all(partial, ("band", "mesh"), 0, 0, axis_index_groups=along_z).sum(0)
    block = block / (NODES * PARTS)
    f_quarter, _ = lax.optimization_barrier((f_quarter, received[0]))
    quarter_rows, mine = exchange(f_quarter.reshape(4, band_rows, NODES // 4), "band", 16, 1)
    quarter_rows, block = lax.optimization_barrier((quarter_rows, block))
    hproj = spread(block, "mesh", PARTS, (1, 2, 4))
    filtered = in_place(quarter_rows, mine).transpose(1, 0, 2).reshape(band_rows, NODES)
    hproj = hproj.reshape(band_rows, 16 * band_rows)
    return filtered, hproj


def solution(mesh):
    placed = (
        P("band", "mesh"),
        P("mesh"),
        P("mesh"),
        P(),
        P("mesh", None),
        P("mesh", None, None),
        P("mesh"),
        P(),
    )
    return jax.shard_map(
        body,
        mesh=mesh,
        in_specs=placed,
        out_specs=(P("band", "mesh"), P("band", None)),
        check_vma=False,
    )
```

```python
import functools

import jax
import jax.numpy as jnp
from jax import lax
from jax.experimental import pallas as pl
from jax.experimental.pallas import tpu as pltpu
from jax.sharding import PartitionSpec as P

DEGREE = 3
OFFSETS = (-2, -1, 1, 2)
HIGHEST = lax.Precision.HIGHEST

PARTS = 32
GROUPS = PARTS // 8
NODES = 2048
SLOTS = 128
GHOSTS = 4 * SLOTS
EXT = GHOSTS + NODES
CELLS = 8
NPC = 343
NPC_PAD = 384
CELL_CHUNKS = NPC_PAD // 128
ENTRIES = CELLS * NPC + GHOSTS
ENTRY_CHUNKS = 26
ENTRY_PAD = ENTRY_CHUNKS * 128
PAD_NODE = 4095
CELL_MULTIPLIER, CELL_SHIFT = 6115, 21
FEW = 5
SKIP = 3
SHORT_RUN = 16
WINDOWS = (
    (3, 8), (4, 11), (6, 13), (7, 16), (8, 19), (10, 21), (11, 24), (12, 26),
    (13, 26), (15, 26), (16, 26), (18, 26), (19, 26), (20, 26), (22, 26), (23, 26),
)

IDX_AT = 0
POS_AT = IDX_AT + CELLS * CELL_CHUNKS
PLACE_AT = POS_AT + ENTRY_CHUNKS
END_AT = PLACE_AT + ENTRY_CHUNKS
SEND_AT = END_AT + EXT // 128
POT_AT = SEND_AT + GHOSTS // 128
MISC_AT = POT_AT + NODES // 128
START_AT = MISC_AT + 4
TABLE_CHUNKS = START_AT + NODES // 128


def groups_of(size, bits):
    mask = sum(bits)
    members = {}
    for i in range(size):
        members.setdefault(i & ~mask, []).append(i)
    return list(members.values())


def spread(block, axis, size, bits):
    members = groups_of(size, bits)
    copies = jnp.broadcast_to(block[None], (len(members[0]),) + block.shape)
    return lax.all_to_all(copies, axis, 0, 0, axis_index_groups=members)


def swapped(block, axis, size, distance):
    return lax.ppermute(block, axis, [(i ^ distance, i) for i in range(size)])


def in_place(blocks, mine):
    return jnp.stack([lax.select_n(mine, *[blocks[j ^ m] for m in range(4)]) for j in range(4)])


def exchange(pieces, axis, size, unit):
    mine = (lax.axis_index(axis) // unit) % 4
    kept, *sent = [lax.dynamic_index_in_dim(pieces, mine ^ d, 0, keepdims=False) for d in range(4)]
    return [kept] + [swapped(p, axis, size, (d + 1) * unit) for d, p in enumerate(sent)], mine


def table_kernel(ordered, slots, send, pot, cell_scale, node_count, out, hot_high, hot_low):
    shape = (32, 128)
    row = lax.broadcasted_iota(jnp.int32, shape, 0)
    lane = lax.broadcasted_iota(jnp.int32, shape, 1)
    order = row * 128 + lane
    valid = order < ENTRIES
    entry = ordered[...] & 4095
    node = ordered[...] >> 12

    def along_rows(x, combine):
        for d in (1, 2, 4, 8, 16, 32, 64):
            x = jnp.where(lane >= d, combine(x, pltpu.roll(x, d, 1)), x)
        ends = jnp.broadcast_to(x[:, 127:128], shape)
        before = jnp.where(row >= 1, pltpu.roll(ends, 1, 0), 0.0)
        for d in (1, 2, 4, 8, 16):
            before = jnp.where(row >= d, combine(before, pltpu.roll(before, d, 0)), before)
        return combine(x, before)

    key = node.astype(jnp.float32)
    shifted = pltpu.roll(key, 1, 1)
    previous = jnp.where(lane == 0, pltpu.roll(shifted, 1, 0), shifted)
    head = (previous != key) | (order == 0)
    at = order.astype(jnp.float32)
    first = along_rows(jnp.where(head, at, 0.0), jnp.maximum)
    place = jnp.where(valid, at - first, 0.0)

    cell = (entry * CELL_MULTIPLIER) >> CELL_SHIFT
    position = entry + jnp.where(entry < CELLS * NPC, cell, CELLS) * (NPC_PAD - NPC)
    position = jnp.where(valid, position, 0).astype(jnp.float32)

    high_row = lax.broadcasted_iota(jnp.int32, (32, 128), 0)
    low_row = lax.broadcasted_iota(jnp.int32, (128, 128), 0)
    for q in range(ENTRY_CHUNKS):
        some = node[q : q + 1, :]
        hot_high[:, chunk(q)] = jnp.where(high_row == (some >> 7), 1.0, 0.0).astype(jnp.bfloat16)
        hot_low[:, chunk(q)] = jnp.where(low_row == (some & 127), 1.0, 0.0).astype(jnp.bfloat16)
    count = lax.dot_general(
        hot_high[...], hot_low[...], (((1,), (1,)), ((), ())), preferred_element_type=jnp.float32
    )
    up_to = along_rows(count, jnp.add)
    end = jnp.where(count > 0.0, up_to - 1.0, -1.0)

    nodes = slots[...]
    nodes = jnp.where(nodes >= NODES, nodes - NODES, nodes + GHOSTS)
    out[IDX_AT:POS_AT, :] = nodes.astype(jnp.float32)
    out[POS_AT:PLACE_AT, :] = position[:ENTRY_CHUNKS]
    out[PLACE_AT:END_AT, :] = place[:ENTRY_CHUNKS]
    out[END_AT:SEND_AT, :] = end[: EXT // 128]
    out[SEND_AT:POT_AT, :] = send[...].astype(jnp.float32)
    out[POT_AT:MISC_AT, :] = pot[...]
    ghost_entries = jnp.broadcast_to(up_to[GHOSTS // 128 - 1 : GHOSTS // 128, 127:128], (1, 128))
    longest = jnp.max(place) + 1.0
    one_lane = lane[:1]
    misc = jnp.where(one_lane == CELLS, node_count[0].astype(jnp.float32), 0.0)
    misc = jnp.where(one_lane == CELLS + 1, ghost_entries, misc)
    misc = jnp.where(one_lane == CELLS + 2, longest, misc)
    out[MISC_AT : MISC_AT + 1, :] = misc
    out[MISC_AT : MISC_AT + 1, 0:CELLS] = cell_scale[...]
    out[MISC_AT + 1 :, :] = jnp.zeros((START_AT - MISC_AT - 1, 128), jnp.float32)


def partition_table(cell_nodes, send_list, potential, cell_scale, node_count):
    shifted = jnp.where(cell_nodes >= NODES, cell_nodes - NODES, cell_nodes + GHOSTS)
    keys = jnp.concatenate([shifted.reshape(-1), send_list.reshape(-1) + GHOSTS])
    ordered = lax.sort(keys * 4096 + lax.iota(jnp.int32, ENTRIES))
    ordered = jnp.pad(ordered, (0, 4096 - ENTRIES), constant_values=PAD_NODE * 4096).reshape(32, 128)
    slots = jnp.pad(cell_nodes, ((0, 0), (0, NPC_PAD - NPC))).reshape(CELLS * CELL_CHUNKS, 128)
    vmem = pl.BlockSpec(memory_space=pltpu.VMEM)
    return pl.pallas_call(
        table_kernel,
        out_shape=jax.ShapeDtypeStruct((START_AT, 128), jnp.float32),
        in_specs=[vmem] * 5 + [pl.BlockSpec(memory_space=pltpu.SMEM)],
        out_specs=vmem,
        scratch_shapes=[
            pltpu.VMEM((32, ENTRY_PAD), jnp.bfloat16),
            pltpu.VMEM((128, ENTRY_PAD), jnp.bfloat16),
        ],
        compiler_params=pltpu.CompilerParams(vmem_limit_bytes=16 * 1024 * 1024),
    )(ordered, slots, send_list, potential.reshape(NODES // 128, 128), cell_scale.reshape(1, CELLS), node_count)


def gathered_tables(own_table, vectors):
    def next_step(both, members, receivers):
        tables, values = both[..., :START_AT, :], both[..., START_AT:, :]
        values = jnp.split(values, receivers, axis=-2)
        operand = jnp.stack([jnp.concatenate([tables, v], axis=-2) for v in values])
        return lax.all_to_all(operand, "mesh", 0, 0, axis_index_groups=groups_of(PARTS, members))

    values = vectors.reshape(PARTS * (NODES // 128), 128)
    both = next_step(jnp.concatenate([own_table, values]), (8, 16), 4)
    both = next_step(both, (2, 4), 4)
    both = next_step(both, (1,), 2)
    return both.transpose(2, 1, 0, 3, 4).reshape(PARTS, TABLE_CHUNKS * 128)


def chunk(c):
    return pl.ds(c * 128, 128)


def rows(g):
    return pl.ds(pl.multiple_of(g * 8, 8), 8)


def picked(sources, index):
    low = index & 127
    high = index >> 7
    total = jnp.zeros((8, 128), jnp.float32)
    for j, source in sources:
        total = jnp.where(high == j, jnp.take_along_axis(source, low, axis=1), total)
    return total


def filter_kernel(
    step_count, last, coef, table, field, matrix, out,
    mat_hi, mat_lo, idx, pos, place, end, send, scale, cur, prev, ext, vals, prod, arrived, w, halo, sums,
):
    lane = lax.broadcasted_iota(jnp.int32, (8, 128), 1)
    last_lane = jnp.full((8, 128), 127, jnp.int32)

    for k in range(CELL_CHUNKS):
        whole = matrix[k * 128 : (k + 1) * 128, :]
        high_part = whole.astype(jnp.bfloat16)
        low_part = (whole - high_part.astype(jnp.float32)).astype(jnp.bfloat16)
        mat_hi[k * 128 : (k + 1) * 128, :] = high_part
        mat_lo[k * 128 : (k + 1) * 128, :] = low_part

    def to_int(dest, first, count):
        for c in range(count):
            dest[:, chunk(c)] = table[:, chunk(first + c)].astype(jnp.int32)

    to_int(idx, IDX_AT, CELLS * CELL_CHUNKS)
    to_int(pos, POS_AT, ENTRY_CHUNKS)
    to_int(place, PLACE_AT, ENTRY_CHUNKS)
    to_int(end, END_AT, EXT // 128)
    to_int(send, SEND_AT, GHOSTS // 128)
    for c in range(CELLS):
        column = table[:, MISC_AT * 128 + c : MISC_AT * 128 + c + 1]
        scale[c * 32 : (c + 1) * 32, :] = jnp.broadcast_to(column, (PARTS, 128))

    def misc(c):
        return table[:, MISC_AT * 128 + CELLS + c : MISC_AT * 128 + CELLS + c + 1]

    short = jnp.max(misc(1)).astype(jnp.int32) <= FEW * 128
    short &= jnp.min(misc(1)).astype(jnp.int32) >= SKIP * 128
    short &= jnp.max(misc(2)).astype(jnp.int32) <= SHORT_RUN
    outside = jnp.zeros((PARTS, 128), jnp.float32)
    for n, (first, stop) in enumerate(WINDOWS):
        ends = table[:, chunk(END_AT + GHOSTS // 128 + n)]
        missed = (ends >= 0.0) & ((ends < first * 128.0) | (ends >= stop * 128.0))
        outside = jnp.maximum(outside, jnp.where(missed, 1.0, 0.0))
    short &= jnp.max(outside).astype(jnp.int32) == 0

    if last:
        for c in range(NODES // 128):
            cur[:, chunk(c)] = field[c // 4 * 32 : (c // 4 + 1) * 32, c % 4, :]
    else:
        live = misc(0).astype(jnp.int32)
        node = lax.broadcasted_iota(jnp.int32, (PARTS, NODES), 1)
        start = table[:, START_AT * 128 : TABLE_CHUNKS * 128]
        cur[...] = jnp.where(node < live, start, 0.0)
        prev[...] = jnp.zeros((PARTS, NODES), jnp.float32)

    def over_groups(body, unroll=1):
        def at(g, _):
            body(g, rows(g))
            return 0

        lax.fori_loop(0, GROUPS, at, 0, unroll=unroll)

    def wrap(values, k):
        c = chunk(k)
        halo[2:34, c] = values
        halo[0:2, c] = values[30:32]
        halo[34:36, c] = values[0:2]

    def products_of(g):
        return [
            (c * CELL_CHUNKS + k, prod[pl.ds(pl.multiple_of(c * 32 + g * 8, 8), 8), chunk(k)])
            for c in range(CELLS)
            for k in range(CELL_CHUNKS)
        ]

    def into_order(r, sources, first, stop):
        for q in range(first, stop):
            w[r, chunk(q)] = picked(sources, pos[r, chunk(q)])

    def partial_runs(places, longest):
        xs = [w[r, chunk(q)] for r, q in places]
        near = [jnp.minimum(place[r, chunk(q)], lane) for r, q in places]
        for d in [1 << k for k in range(7) if (1 << k) < longest]:
            back = (lane - d) & 127
            moved = [jnp.take_along_axis(x, back, axis=1) for x in xs]
            xs = [x + jnp.where(a >= d, m, 0.0) for x, a, m in zip(xs, near, moved)]
        for (r, q), x in zip(places, xs):
            w[r, chunk(q)] = x

    def joined_runs(r, first, stop):
        xs = [w[r, chunk(q)] for q in range(first, stop)]
        done = [(first, xs[0])]
        for q, x, before in zip(range(first + 1, stop), xs[1:], xs):
            carry = jnp.take_along_axis(before, last_lane, axis=1)
            done.append((q, x + jnp.where(place[r, chunk(q)] > lane, carry, 0.0)))
        return done

    def chained_runs(r):
        carry = jnp.zeros((8, 128), jnp.float32)
        done = []
        for q in range(ENTRY_CHUNKS):
            x = w[r, chunk(q)]
            total = jnp.take_along_axis(x, last_lane, axis=1)
            goes_on = place[r, chunk(q)] > lane
            through = jnp.take_along_axis(jnp.where(goes_on, 1.0, 0.0), last_lane, axis=1)
            done.append((q, x + jnp.where(goes_on, carry, 0.0)))
            carry = total + through * carry
        return done

    def run_ends(r, sources, node_first, windows):
        for n, (first, stop) in enumerate(windows):
            inside = [(q, source) for q, source in sources if first <= q < stop]
            sums[r, chunk(n)] = picked(inside, end[r, chunk(node_first + n)])

    anywhere = ((0, ENTRY_CHUNKS),)

    def with_arrivals(g, r):
        base = CELLS * CELL_CHUNKS
        return products_of(g) + [(base + k, arrived[r, chunk(k)]) for k in range(4)]

    fixed = [pl.ds(g * 8, 8) for g in range(GROUPS)]

    def in_order_and_summed(sources_of):
        def at(g, r):
            into_order(r, sources_of(g, r), 0, ENTRY_CHUNKS)
            partial_runs([(r, q) for q in range(ENTRY_CHUNKS)], 128)

        over_groups(at)

    def ghost_sums():
        for g, r in enumerate(fixed):
            into_order(r, products_of(g), 0, FEW)
        partial_runs([(r, q) for r in fixed for q in range(FEW)], SHORT_RUN)
        for r in fixed:
            run_ends(r, joined_runs(r, 0, FEW), 0, ((0, FEW),) * 4)

    def ghost_sums_any():
        in_order_and_summed(lambda g, r: products_of(g))
        over_groups(lambda g, r: run_ends(r, chained_runs(r), 0, anywhere * 4))

    def own_sums():
        over_groups(lambda g, r: into_order(r, with_arrivals(g, r), SKIP, ENTRY_CHUNKS), 2)
        for r in fixed:
            partial_runs([(r, q) for q in range(SKIP, ENTRY_CHUNKS)], SHORT_RUN)
        over_groups(lambda g, r: run_ends(r, joined_runs(r, SKIP, ENTRY_CHUNKS), 4, WINDOWS), 2)

    def own_sums_any():
        in_order_and_summed(with_arrivals)
        over_groups(lambda g, r: run_ends(r, chained_runs(r), 4, anywhere * 16))

    def apply():
        def outgoing(g, r):
            sources = [(j, cur[r, chunk(j)]) for j in range(NODES // 128)]
            for k in range(4):
                sums[r, chunk(k)] = picked(sources, send[r, chunk(k)])

        for g in range(GROUPS):
            outgoing(g, pl.ds(g * 8, 8))
        for k in range(4):
            wrap(sums[:, k * 128 : (k + 1) * 128], k)
        for k, o in enumerate(OFFSETS):
            ext[:, k * 128 : (k + 1) * 128] = halo[2 + o : 34 + o, k * 128 : (k + 1) * 128]
        ext[:, GHOSTS:] = cur[...]

        def gather(g, r):
            sources = [(j, ext[r, chunk(j)]) for j in range(EXT // 128)]

            for c in range(CELLS):
                there = pl.ds(pl.multiple_of(c * 32 + g * 8, 8), 8)
                for k in range(CELL_CHUNKS):
                    vals[there, chunk(k)] = picked(sources, idx[r, chunk(c * CELL_CHUNKS + k)])

        over_groups(gather, 2)

        x = vals[...]
        high = x.astype(jnp.bfloat16)
        low = (x - high.astype(jnp.float32)).astype(jnp.bfloat16)

        def dot(a, b):
            return jnp.dot(a, b, preferred_element_type=jnp.float32)

        y = dot(high, mat_hi[...]) + (dot(low, mat_hi[...]) + dot(high, mat_lo[...]))
        for k in range(CELL_CHUNKS):
            prod[:, k * 128 : (k + 1) * 128] = y[:, k * 128 : (k + 1) * 128] * scale[...]

        pl.when(short)(ghost_sums)
        pl.when(~short)(ghost_sums_any)
        for k in range(4):
            wrap(sums[:, k * 128 : (k + 1) * 128], k)
        for k, o in enumerate(OFFSETS):
            arrived[:, k * 128 : (k + 1) * 128] = halo[2 - o : 34 - o, k * 128 : (k + 1) * 128]

        pl.when(short)(own_sums)
        pl.when(~short)(own_sums_any)

    def step(i, _):
        apply()
        degree = lax.rem(i, DEGREE)
        gain = coef[degree]
        back = coef[DEGREE + degree]
        centre = coef[2 * DEGREE]
        for c in range(NODES // 128):
            here = chunk(c)
            v = cur[:, here]
            hv = sums[:, here] + table[:, chunk(POT_AT + c)] * v
            following = gain * (hv - centre * v)
            following = jnp.where(degree == 0, following, following - back * prev[:, here])
            prev[:, here] = v
            cur[:, here] = following
        return 0

    if last:
        apply()
        for c in range(NODES // 128):
            cur[:, chunk(c)] = sums[:, chunk(c)] + table[:, chunk(POT_AT + c)] * cur[:, chunk(c)]
    else:
        lax.fori_loop(0, step_count, step, 0)
    for c in range(NODES // 128):
        out[c // 4 * 32 : (c // 4 + 1) * 32, c % 4, :] = cur[:, chunk(c)]


def run_filter(coef, table, field, cell_matrix, step_count, last):
    padded = jnp.pad(cell_matrix, ((0, NPC_PAD - NPC), (0, NPC_PAD - NPC)))
    vmem = pl.BlockSpec(memory_space=pltpu.VMEM)
    f32, i32 = jnp.float32, jnp.int32
    cells = CELLS * PARTS
    return pl.pallas_call(
        functools.partial(filter_kernel, step_count, last),
        out_shape=jax.ShapeDtypeStruct((4 * PARTS, NODES // 512, 128), f32),
        in_specs=[pl.BlockSpec(memory_space=pltpu.SMEM)] + [vmem] * 3,
        out_specs=vmem,
        scratch_shapes=[
            pltpu.VMEM((NPC_PAD, NPC_PAD), jnp.bfloat16),
            pltpu.VMEM((NPC_PAD, NPC_PAD), jnp.bfloat16),
            pltpu.VMEM((PARTS, CELLS * NPC_PAD), i32),
            pltpu.VMEM((PARTS, ENTRY_PAD), i32),
            pltpu.VMEM((PARTS, ENTRY_PAD), i32),
            pltpu.VMEM((PARTS, EXT), i32),
            pltpu.VMEM((PARTS, GHOSTS), i32),
            pltpu.VMEM((cells, 128), f32),
            pltpu.VMEM((PARTS, NODES), f32),
            pltpu.VMEM((PARTS, NODES), f32),
            pltpu.VMEM((PARTS, EXT), f32),
            pltpu.VMEM((cells, NPC_PAD), f32),
            pltpu.VMEM((cells, NPC_PAD), f32),
            pltpu.VMEM((PARTS, GHOSTS), f32),
            pltpu.VMEM((PARTS, ENTRY_PAD), f32),
            pltpu.VMEM((40, GHOSTS), f32),
            pltpu.VMEM((PARTS, NODES), f32),
        ],
        compiler_params=pltpu.CompilerParams(vmem_limit_bytes=48 * 1024 * 1024),
        cost_estimate=pl.CostEstimate(
            flops=step_count * 15_000_000_000, bytes_accessed=step_count * 50_000_000, transcendentals=0
        ),
    )(coef, table, field, padded)


def coefficients(filter_bounds):
    lowest, wanted_top, upper = filter_bounds[0], filter_bounds[1], filter_bounds[2]
    half_width = (upper - wanted_top) / 2.0
    centre = (upper + wanted_top) / 2.0
    sigma = half_width / (lowest - centre)
    ratio = 2.0 / sigma
    gains, backs = [sigma / half_width], [jnp.zeros_like(sigma)]
    for _ in range(DEGREE - 1):
        following = 1.0 / (ratio - sigma)
        gains.append(2.0 * following / half_width)
        backs.append(sigma * following)
        sigma = following
    return jnp.stack(gains + backs + [centre, centre])


def body(vectors, potential, cell_scale, cell_matrix, cell_nodes, send_list, node_count, filter_bounds):
    own_table = partition_table(cell_nodes, send_list[0], potential, cell_scale, node_count)
    table = gathered_tables(own_table, vectors)

    coef = coefficients(filter_bounds)
    quarters = groups_of(16 * PARTS, (1, 2, 4, 8, 16, PARTS, 2 * PARTS))

    def to_quarters(field):
        pieces = lax.all_to_all(field, ("band", "mesh"), 0, 0, axis_index_groups=quarters)
        return pieces.reshape(4 * PARTS, NODES // 4)

    f = run_filter(coef, table, jnp.zeros((8, 128), jnp.float32), cell_matrix, 2 * DEGREE, False)
    f_quarter = to_quarters(f)
    g = run_filter(coef, table, f, cell_matrix, 1, True)
    left = to_quarters(g)
    band_rows = vectors.shape[0]
    received = [swapped(f_quarter, "band", 16, 4 * d) for d in (1, 2, 3)]
    products = [
        lax.dot_general(left, right, (((1,), (1,)), ((), ())), precision=HIGHEST)
        for right in (f_quarter, *received)
    ]
    partial = in_place(products, lax.axis_index("band") // 4)

    plane = groups_of(PARTS, (1, 2, 4))
    partial = partial.reshape(4, 4, 8, band_rows // 8, 4 * band_rows).transpose(2, 1, 3, 0, 4)
    partial = partial.reshape(8, 4, band_rows // 8, 16 * band_rows)
    partial = lax.all_to_all(partial, "mesh", 0, 0, axis_index_groups=plane).sum(0)
    along_z = groups_of(16 * PARTS, (8, 16, PARTS, 2 * PARTS))
    partial = jnp.broadcast_to(partial[:, None], (4, 4) + partial.shape[1:])
    partial = partial.reshape((16,) + partial.shape[2:])
    block = lax.all_to_all(partial, ("band", "mesh"), 0, 0, axis_index_groups=along_z).sum(0)
    block = block / (NODES * PARTS)
    f_quarter, _ = lax.optimization_barrier((f_quarter, received[0]))
    quarter_rows, mine = exchange(f_quarter.reshape(4, band_rows, NODES // 4), "band", 16, 1)
    quarter_rows, block = lax.optimization_barrier((quarter_rows, block))
    hproj = spread(block, "mesh", PARTS, (1, 2, 4))
    filtered = in_place(quarter_rows, mine).transpose(1, 0, 2).reshape(band_rows, NODES)
    hproj = hproj.reshape(band_rows, 16 * band_rows)
    return filtered, hproj


def solution(mesh):
    placed = (
        P("band", "mesh"),
        P("mesh"),
        P("mesh"),
        P(),
        P("mesh", None),
        P("mesh", None, None),
        P("mesh"),
        P(),
    )
    return jax.shard_map(
        body,
        mesh=mesh,
        in_specs=placed,
        out_specs=(P("band", "mesh"), P("band", None)),
        check_vma=False,
    )
```

```python
import functools

import jax
import jax.numpy as jnp
from jax import lax
from jax.experimental import pallas as pl
from jax.experimental.pallas import tpu as pltpu
from jax.sharding import PartitionSpec as P

DEGREE = 3
OFFSETS = (-2, -1, 1, 2)
HIGHEST = lax.Precision.HIGHEST

PARTS = 32
GROUPS = PARTS // 8
NODES = 2048
SLOTS = 128
GHOSTS = 4 * SLOTS
EXT = GHOSTS + NODES
CELLS = 8
NPC = 343
NPC_PAD = 384
CELL_CHUNKS = NPC_PAD // 128
ENTRIES = CELLS * NPC + GHOSTS
ENTRY_CHUNKS = 26
ENTRY_PAD = ENTRY_CHUNKS * 128
PAD_NODE = 4095
CELL_MULTIPLIER, CELL_SHIFT = 6115, 21
FEW = 5
SKIP = 3
SHORT_RUN = 16
WINDOWS = (
    (3, 8), (4, 11), (6, 13), (7, 16), (8, 19), (10, 21), (11, 24), (12, 26),
    (13, 26), (15, 26), (16, 26), (18, 26), (19, 26), (20, 26), (22, 26), (23, 26),
)

IDX_AT = 0
POS_AT = IDX_AT + CELLS * CELL_CHUNKS
PLACE_AT = POS_AT + ENTRY_CHUNKS
END_AT = PLACE_AT + ENTRY_CHUNKS
SEND_AT = END_AT + EXT // 128
POT_AT = SEND_AT + GHOSTS // 128
MISC_AT = POT_AT + NODES // 128
START_AT = MISC_AT + 4
TABLE_CHUNKS = START_AT + NODES // 128


def groups_of(size, bits):
    mask = sum(bits)
    members = {}
    for i in range(size):
        members.setdefault(i & ~mask, []).append(i)
    return list(members.values())


def spread(block, axis, size, bits):
    members = groups_of(size, bits)
    copies = jnp.broadcast_to(block[None], (len(members[0]),) + block.shape)
    return lax.all_to_all(copies, axis, 0, 0, axis_index_groups=members)


def swapped(block, axis, size, distance):
    return lax.ppermute(block, axis, [(i ^ distance, i) for i in range(size)])


def in_place(blocks, mine):
    return jnp.stack([lax.select_n(mine, *[blocks[j ^ m] for m in range(4)]) for j in range(4)])


def exchange(pieces, axis, size, unit):
    mine = (lax.axis_index(axis) // unit) % 4
    kept, *sent = [lax.dynamic_index_in_dim(pieces, mine ^ d, 0, keepdims=False) for d in range(4)]
    return [kept] + [swapped(p, axis, size, (d + 1) * unit) for d, p in enumerate(sent)], mine


def table_kernel(ordered, slots, send, pot, cell_scale, node_count, out, hot_high, hot_low):
    shape = (32, 128)
    row = lax.broadcasted_iota(jnp.int32, shape, 0)
    lane = lax.broadcasted_iota(jnp.int32, shape, 1)
    order = row * 128 + lane
    valid = order < ENTRIES
    entry = ordered[...] & 4095
    node = ordered[...] >> 12

    def along_rows(x, combine):
        for d in (1, 2, 4, 8, 16, 32, 64):
            x = jnp.where(lane >= d, combine(x, pltpu.roll(x, d, 1)), x)
        ends = jnp.broadcast_to(x[:, 127:128], shape)
        before = jnp.where(row >= 1, pltpu.roll(ends, 1, 0), 0.0)
        for d in (1, 2, 4, 8, 16):
            before = jnp.where(row >= d, combine(before, pltpu.roll(before, d, 0)), before)
        return combine(x, before)

    key = node.astype(jnp.float32)
    shifted = pltpu.roll(key, 1, 1)
    previous = jnp.where(lane == 0, pltpu.roll(shifted, 1, 0), shifted)
    head = (previous != key) | (order == 0)
    at = order.astype(jnp.float32)
    first = along_rows(jnp.where(head, at, 0.0), jnp.maximum)
    place = jnp.where(valid, at - first, 0.0)

    cell = (entry * CELL_MULTIPLIER) >> CELL_SHIFT
    position = entry + jnp.where(entry < CELLS * NPC, cell, CELLS) * (NPC_PAD - NPC)
    position = jnp.where(valid, position, 0).astype(jnp.float32)

    high_row = lax.broadcasted_iota(jnp.int32, (32, 128), 0)
    low_row = lax.broadcasted_iota(jnp.int32, (128, 128), 0)
    for q in range(ENTRY_CHUNKS):
        some = node[q : q + 1, :]
        hot_high[:, chunk(q)] = jnp.where(high_row == (some >> 7), 1.0, 0.0).astype(jnp.bfloat16)
        hot_low[:, chunk(q)] = jnp.where(low_row == (some & 127), 1.0, 0.0).astype(jnp.bfloat16)
    count = lax.dot_general(
        hot_high[...], hot_low[...], (((1,), (1,)), ((), ())), preferred_element_type=jnp.float32
    )
    up_to = along_rows(count, jnp.add)
    end = jnp.where(count > 0.0, up_to - 1.0, -1.0)

    out[IDX_AT:POS_AT, :] = slots[...].astype(jnp.float32)
    out[POS_AT:PLACE_AT, :] = position[:ENTRY_CHUNKS]
    out[PLACE_AT:END_AT, :] = place[:ENTRY_CHUNKS]
    out[END_AT:SEND_AT, :] = end[: EXT // 128]
    out[SEND_AT:POT_AT, :] = (send[...] - GHOSTS).astype(jnp.float32)
    out[POT_AT:MISC_AT, :] = pot[...]
    ghost_entries = jnp.broadcast_to(up_to[GHOSTS // 128 - 1 : GHOSTS // 128, 127:128], (1, 128))
    longest = jnp.max(place) + 1.0
    one_lane = lane[:1]
    misc = jnp.where(one_lane == CELLS, node_count[0].astype(jnp.float32), 0.0)
    misc = jnp.where(one_lane == CELLS + 1, ghost_entries, misc)
    misc = jnp.where(one_lane == CELLS + 2, longest, misc)
    out[MISC_AT : MISC_AT + 1, :] = misc
    out[MISC_AT : MISC_AT + 1, 0:CELLS] = cell_scale[...]
    out[MISC_AT + 1 :, :] = jnp.zeros((START_AT - MISC_AT - 1, 128), jnp.float32)


def partition_table(cell_nodes, send_list, potential, cell_scale, node_count):
    shifted = jnp.where(cell_nodes >= NODES, cell_nodes - NODES, cell_nodes + GHOSTS)
    send = send_list + GHOSTS
    keys = jnp.concatenate([shifted.reshape(-1), send.reshape(-1)])
    ordered = lax.sort(keys * 4096 + lax.iota(jnp.int32, ENTRIES))
    ordered = jnp.pad(ordered, (0, 4096 - ENTRIES), constant_values=PAD_NODE * 4096).reshape(32, 128)
    slots = jnp.pad(shifted, ((0, 0), (0, NPC_PAD - NPC))).reshape(CELLS * CELL_CHUNKS, 128)
    vmem = pl.BlockSpec(memory_space=pltpu.VMEM)
    return pl.pallas_call(
        table_kernel,
        out_shape=jax.ShapeDtypeStruct((START_AT, 128), jnp.float32),
        in_specs=[vmem] * 5 + [pl.BlockSpec(memory_space=pltpu.SMEM)],
        out_specs=vmem,
        scratch_shapes=[
            pltpu.VMEM((32, ENTRY_PAD), jnp.bfloat16),
            pltpu.VMEM((128, ENTRY_PAD), jnp.bfloat16),
        ],
        compiler_params=pltpu.CompilerParams(vmem_limit_bytes=16 * 1024 * 1024),
    )(ordered, slots, send, potential.reshape(NODES // 128, 128), cell_scale.reshape(1, CELLS), node_count)


def gathered_tables(own_table, vectors):
    def next_step(both, members, receivers):
        tables, values = both[..., :START_AT, :], both[..., START_AT:, :]
        values = jnp.split(values, receivers, axis=-2)
        operand = jnp.stack([jnp.concatenate([tables, v], axis=-2) for v in values])
        return lax.all_to_all(operand, "mesh", 0, 0, axis_index_groups=groups_of(PARTS, members))

    values = vectors.reshape(PARTS * (NODES // 128), 128)
    both = next_step(jnp.concatenate([own_table, values]), (8, 16), 4)
    both = next_step(both, (2, 4), 4)
    both = next_step(both, (1,), 2)
    return both.transpose(2, 1, 0, 3, 4).reshape(PARTS, TABLE_CHUNKS * 128)


def chunk(c):
    return pl.ds(c * 128, 128)


def rows(g):
    return pl.ds(pl.multiple_of(g * 8, 8), 8)


def picked(sources, index):
    low = index & 127
    high = index >> 7
    total = jnp.zeros((8, 128), jnp.float32)
    for j, source in sources:
        total = jnp.where(high == j, jnp.take_along_axis(source, low, axis=1), total)
    return total


def filter_kernel(
    step_count, last, coef, table, field, matrix, out,
    mat_hi, mat_lo, idx, pos, place, end, send, scale, cur, prev, ext, vals, prod, arrived, w, halo, sums,
):
    lane = lax.broadcasted_iota(jnp.int32, (8, 128), 1)
    last_lane = jnp.full((8, 128), 127, jnp.int32)

    for k in range(CELL_CHUNKS):
        whole = matrix[k * 128 : (k + 1) * 128, :]
        high_part = whole.astype(jnp.bfloat16)
        low_part = (whole - high_part.astype(jnp.float32)).astype(jnp.bfloat16)
        mat_hi[k * 128 : (k + 1) * 128, :] = high_part
        mat_lo[k * 128 : (k + 1) * 128, :] = low_part

    def to_int(dest, first, count):
        for c in range(count):
            dest[:, chunk(c)] = table[:, chunk(first + c)].astype(jnp.int32)

    to_int(idx, IDX_AT, CELLS * CELL_CHUNKS)
    to_int(pos, POS_AT, ENTRY_CHUNKS)
    to_int(place, PLACE_AT, ENTRY_CHUNKS)
    to_int(end, END_AT, EXT // 128)
    to_int(send, SEND_AT, GHOSTS // 128)
    for c in range(CELLS):
        column = table[:, MISC_AT * 128 + c : MISC_AT * 128 + c + 1]
        scale[c * 32 : (c + 1) * 32, :] = jnp.broadcast_to(column, (PARTS, 128))

    def misc(c):
        return table[:, MISC_AT * 128 + CELLS + c : MISC_AT * 128 + CELLS + c + 1]

    short = jnp.max(misc(1)).astype(jnp.int32) <= FEW * 128
    short &= jnp.min(misc(1)).astype(jnp.int32) >= SKIP * 128
    short &= jnp.max(misc(2)).astype(jnp.int32) <= SHORT_RUN
    outside = jnp.zeros((PARTS, 128), jnp.float32)
    for n, (first, stop) in enumerate(WINDOWS):
        ends = table[:, chunk(END_AT + GHOSTS // 128 + n)]
        missed = (ends >= 0.0) & ((ends < first * 128.0) | (ends >= stop * 128.0))
        outside = jnp.maximum(outside, jnp.where(missed, 1.0, 0.0))
    short &= jnp.max(outside).astype(jnp.int32) == 0

    if last:
        for c in range(NODES // 128):
            cur[:, chunk(c)] = field[c // 4 * 32 : (c // 4 + 1) * 32, c % 4, :]
    else:
        live = misc(0).astype(jnp.int32)
        node = lax.broadcasted_iota(jnp.int32, (PARTS, NODES), 1)
        start = table[:, START_AT * 128 : TABLE_CHUNKS * 128]
        cur[...] = jnp.where(node < live, start, 0.0)
        prev[...] = jnp.zeros((PARTS, NODES), jnp.float32)

    def over_groups(body, unroll=1):
        def at(g, _):
            body(g, rows(g))
            return 0

        lax.fori_loop(0, GROUPS, at, 0, unroll=unroll)

    def wrap(values, k):
        c = chunk(k)
        halo[2:34, c] = values
        halo[0:2, c] = values[30:32]
        halo[34:36, c] = values[0:2]

    def products_of(g):
        return [
            (c * CELL_CHUNKS + k, prod[pl.ds(pl.multiple_of(c * 32 + g * 8, 8), 8), chunk(k)])
            for c in range(CELLS)
            for k in range(CELL_CHUNKS)
        ]

    def into_order(r, sources, first, stop):
        for q in range(first, stop):
            w[r, chunk(q)] = picked(sources, pos[r, chunk(q)])

    def partial_runs(places, longest):
        xs = [w[r, chunk(q)] for r, q in places]
        near = [jnp.minimum(place[r, chunk(q)], lane) for r, q in places]
        for d in [1 << k for k in range(7) if (1 << k) < longest]:
            back = (lane - d) & 127
            moved = [jnp.take_along_axis(x, back, axis=1) for x in xs]
            xs = [x + jnp.where(a >= d, m, 0.0) for x, a, m in zip(xs, near, moved)]
        for (r, q), x in zip(places, xs):
            w[r, chunk(q)] = x

    def joined_runs(r, first, stop):
        xs = [w[r, chunk(q)] for q in range(first, stop)]
        done = [(first, xs[0])]
        for q, x, before in zip(range(first + 1, stop), xs[1:], xs):
            carry = jnp.take_along_axis(before, last_lane, axis=1)
            done.append((q, x + jnp.where(place[r, chunk(q)] > lane, carry, 0.0)))
        return done

    def chained_runs(r):
        carry = jnp.zeros((8, 128), jnp.float32)
        done = []
        for q in range(ENTRY_CHUNKS):
            x = w[r, chunk(q)]
            total = jnp.take_along_axis(x, last_lane, axis=1)
            goes_on = place[r, chunk(q)] > lane
            through = jnp.take_along_axis(jnp.where(goes_on, 1.0, 0.0), last_lane, axis=1)
            done.append((q, x + jnp.where(goes_on, carry, 0.0)))
            carry = total + through * carry
        return done

    def run_ends(r, sources, node_first, windows):
        for n, (first, stop) in enumerate(windows):
            inside = [(q, source) for q, source in sources if first <= q < stop]
            sums[r, chunk(n)] = picked(inside, end[r, chunk(node_first + n)])

    anywhere = ((0, ENTRY_CHUNKS),)

    def with_arrivals(g, r):
        base = CELLS * CELL_CHUNKS
        return products_of(g) + [(base + k, arrived[r, chunk(k)]) for k in range(4)]

    fixed = [pl.ds(g * 8, 8) for g in range(GROUPS)]

    def in_order_and_summed(sources_of):
        def at(g, r):
            into_order(r, sources_of(g, r), 0, ENTRY_CHUNKS)
            partial_runs([(r, q) for q in range(ENTRY_CHUNKS)], 128)

        over_groups(at)

    def ghost_sums():
        for g, r in enumerate(fixed):
            into_order(r, products_of(g), 0, FEW)
        partial_runs([(r, q) for r in fixed for q in range(FEW)], SHORT_RUN)
        for r in fixed:
            run_ends(r, joined_runs(r, 0, FEW), 0, ((0, FEW),) * 4)

    def ghost_sums_any():
        in_order_and_summed(lambda g, r: products_of(g))
        over_groups(lambda g, r: run_ends(r, chained_runs(r), 0, anywhere * 4))

    def own_sums():
        over_groups(lambda g, r: into_order(r, with_arrivals(g, r), SKIP, ENTRY_CHUNKS), 2)
        for r in fixed:
            partial_runs([(r, q) for q in range(SKIP, ENTRY_CHUNKS)], SHORT_RUN)
        over_groups(lambda g, r: run_ends(r, joined_runs(r, SKIP, ENTRY_CHUNKS), 4, WINDOWS), 2)

    def own_sums_any():
        in_order_and_summed(with_arrivals)
        over_groups(lambda g, r: run_ends(r, chained_runs(r), 4, anywhere * 16))

    def apply():
        def outgoing(g, r):
            sources = [(j, cur[r, chunk(j)]) for j in range(NODES // 128)]
            for k in range(4):
                sums[r, chunk(k)] = picked(sources, send[r, chunk(k)])

        for g in range(GROUPS):
            outgoing(g, pl.ds(g * 8, 8))
        for k in range(4):
            wrap(sums[:, k * 128 : (k + 1) * 128], k)
        for k, o in enumerate(OFFSETS):
            ext[:, k * 128 : (k + 1) * 128] = halo[2 + o : 34 + o, k * 128 : (k + 1) * 128]
        ext[:, GHOSTS:] = cur[...]

        def gather(g, r):
            sources = [(j, ext[r, chunk(j)]) for j in range(EXT // 128)]

            for c in range(CELLS):
                there = pl.ds(pl.multiple_of(c * 32 + g * 8, 8), 8)
                for k in range(CELL_CHUNKS):
                    vals[there, chunk(k)] = picked(sources, idx[r, chunk(c * CELL_CHUNKS + k)])

        over_groups(gather, 2)

        x = vals[...]
        high = x.astype(jnp.bfloat16)
        low = (x - high.astype(jnp.float32)).astype(jnp.bfloat16)

        def dot(a, b):
            return jnp.dot(a, b, preferred_element_type=jnp.float32)

        y = dot(high, mat_hi[...]) + (dot(low, mat_hi[...]) + dot(high, mat_lo[...]))
        for k in range(CELL_CHUNKS):
            prod[:, k * 128 : (k + 1) * 128] = y[:, k * 128 : (k + 1) * 128] * scale[...]

        pl.when(short)(ghost_sums)
        pl.when(~short)(ghost_sums_any)
        for k in range(4):
            wrap(sums[:, k * 128 : (k + 1) * 128], k)
        for k, o in enumerate(OFFSETS):
            arrived[:, k * 128 : (k + 1) * 128] = halo[2 - o : 34 - o, k * 128 : (k + 1) * 128]

        pl.when(short)(own_sums)
        pl.when(~short)(own_sums_any)

    def step(i, _):
        apply()
        degree = lax.rem(i, DEGREE)
        gain = coef[degree]
        back = coef[DEGREE + degree]
        centre = coef[2 * DEGREE]
        for c in range(NODES // 128):
            here = chunk(c)
            v = cur[:, here]
            hv = sums[:, here] + table[:, chunk(POT_AT + c)] * v
            following = gain * (hv - centre * v)
            following = jnp.where(degree == 0, following, following - back * prev[:, here])
            prev[:, here] = v
            cur[:, here] = following
        return 0

    if last:
        apply()
        for c in range(NODES // 128):
            cur[:, chunk(c)] = sums[:, chunk(c)] + table[:, chunk(POT_AT + c)] * cur[:, chunk(c)]
    else:
        lax.fori_loop(0, step_count, step, 0)
    for c in range(NODES // 128):
        out[c // 4 * 32 : (c // 4 + 1) * 32, c % 4, :] = cur[:, chunk(c)]


def run_filter(coef, table, field, cell_matrix, step_count, last):
    padded = jnp.pad(cell_matrix, ((0, NPC_PAD - NPC), (0, NPC_PAD - NPC)))
    vmem = pl.BlockSpec(memory_space=pltpu.VMEM)
    f32, i32 = jnp.float32, jnp.int32
    cells = CELLS * PARTS
    return pl.pallas_call(
        functools.partial(filter_kernel, step_count, last),
        out_shape=jax.ShapeDtypeStruct((4 * PARTS, NODES // 512, 128), f32),
        in_specs=[pl.BlockSpec(memory_space=pltpu.SMEM)] + [vmem] * 3,
        out_specs=vmem,
        scratch_shapes=[
            pltpu.VMEM((NPC_PAD, NPC_PAD), jnp.bfloat16),
            pltpu.VMEM((NPC_PAD, NPC_PAD), jnp.bfloat16),
            pltpu.VMEM((PARTS, CELLS * NPC_PAD), i32),
            pltpu.VMEM((PARTS, ENTRY_PAD), i32),
            pltpu.VMEM((PARTS, ENTRY_PAD), i32),
            pltpu.VMEM((PARTS, EXT), i32),
            pltpu.VMEM((PARTS, GHOSTS), i32),
            pltpu.VMEM((cells, 128), f32),
            pltpu.VMEM((PARTS, NODES), f32),
            pltpu.VMEM((PARTS, NODES), f32),
            pltpu.VMEM((PARTS, EXT), f32),
            pltpu.VMEM((cells, NPC_PAD), f32),
            pltpu.VMEM((cells, NPC_PAD), f32),
            pltpu.VMEM((PARTS, GHOSTS), f32),
            pltpu.VMEM((PARTS, ENTRY_PAD), f32),
            pltpu.VMEM((40, GHOSTS), f32),
            pltpu.VMEM((PARTS, NODES), f32),
        ],
        compiler_params=pltpu.CompilerParams(vmem_limit_bytes=48 * 1024 * 1024),
        cost_estimate=pl.CostEstimate(
            flops=step_count * 15_000_000_000, bytes_accessed=step_count * 50_000_000, transcendentals=0
        ),
    )(coef, table, field, padded)


def coefficients(filter_bounds):
    lowest, wanted_top, upper = filter_bounds[0], filter_bounds[1], filter_bounds[2]
    half_width = (upper - wanted_top) / 2.0
    centre = (upper + wanted_top) / 2.0
    sigma = half_width / (lowest - centre)
    ratio = 2.0 / sigma
    gains, backs = [sigma / half_width], [jnp.zeros_like(sigma)]
    for _ in range(DEGREE - 1):
        following = 1.0 / (ratio - sigma)
        gains.append(2.0 * following / half_width)
        backs.append(sigma * following)
        sigma = following
    return jnp.stack(gains + backs + [centre, centre])


def body(vectors, potential, cell_scale, cell_matrix, cell_nodes, send_list, node_count, filter_bounds):
    own_table = partition_table(cell_nodes, send_list[0], potential, cell_scale, node_count)
    table = gathered_tables(own_table, vectors)

    coef = coefficients(filter_bounds)
    quarters = groups_of(16 * PARTS, (1, 2, 4, 8, 16, PARTS, 2 * PARTS))

    def to_quarters(field):
        pieces = lax.all_to_all(field, ("band", "mesh"), 0, 0, axis_index_groups=quarters)
        return pieces.reshape(4 * PARTS, NODES // 4)

    f = run_filter(coef, table, jnp.zeros((8, 128), jnp.float32), cell_matrix, 2 * DEGREE, False)
    f_quarter = to_quarters(f)
    g = run_filter(coef, table, f, cell_matrix, 1, True)
    left = to_quarters(g)
    band_rows = vectors.shape[0]
    received = [swapped(f_quarter, "band", 16, 4 * d) for d in (1, 2, 3)]
    products = [
        lax.dot_general(left, right, (((1,), (1,)), ((), ())), precision=HIGHEST)
        for right in (f_quarter, *received)
    ]
    partial = in_place(products, lax.axis_index("band") // 4)

    plane = groups_of(PARTS, (1, 2, 4))
    partial = partial.reshape(4, 4, 8, band_rows // 8, 4 * band_rows).transpose(2, 1, 3, 0, 4)
    partial = partial.reshape(8, 4, band_rows // 8, 16 * band_rows)
    partial = lax.all_to_all(partial, "mesh", 0, 0, axis_index_groups=plane).sum(0)
    along_z = groups_of(16 * PARTS, (8, 16, PARTS, 2 * PARTS))
    partial = jnp.broadcast_to(partial[:, None], (4, 4) + partial.shape[1:])
    partial = partial.reshape((16,) + partial.shape[2:])
    block = lax.all_to_all(partial, ("band", "mesh"), 0, 0, axis_index_groups=along_z).sum(0)
    block = block / (NODES * PARTS)
    f_quarter, _ = lax.optimization_barrier((f_quarter, received[0]))
    quarter_rows, mine = exchange(f_quarter.reshape(4, band_rows, NODES // 4), "band", 16, 1)
    quarter_rows, block = lax.optimization_barrier((quarter_rows, block))
    hproj = spread(block, "mesh", PARTS, (1, 2, 4))
    filtered = in_place(quarter_rows, mine).transpose(1, 0, 2).reshape(band_rows, NODES)
    hproj = hproj.reshape(band_rows, 16 * band_rows)
    return filtered, hproj


def solution(mesh):
    placed = (
        P("band", "mesh"),
        P("mesh"),
        P("mesh"),
        P(),
        P("mesh", None),
        P("mesh", None, None),
        P("mesh"),
        P(),
    )
    return jax.shard_map(
        body,
        mesh=mesh,
        in_specs=placed,
        out_specs=(P("band", "mesh"), P("band", None)),
        check_vma=False,
    )
```
